256 devices in a mesh: row: 16 (over z, y_lo), col: 16 (over x, y_hi, core).
Axes of the slice: x: 4, y: 4 (y_hi: 2, y_lo: 2; y = y_hi * 2 + y_lo), z: 8, core: 2. Of those that a mesh axis runs over, the one named last changes fastest.
Arguments:
- pair: bfloat16 [384, 384, 128], P('row', 'col'), may hold values from -6 to 6
- cotangent: bfloat16 [384, 384, 128], P('row', 'col'), may hold values from -6 to 6
- w_in: bfloat16 [128, 640], replicated, may hold values from -0.5 to 0.5
- w_out: bfloat16 [128, 128], replicated, may hold values from -0.5 to 0.5
- norm_params: float32 [4, 128], replicated, may hold values from 0.1 to 1.9
Outputs:
- update: bfloat16 [384, 384, 128], P('row', 'col')
- grad_pair: bfloat16 [384, 384, 128], P('row', 'col')
- grad_w_in: float32 [128, 640], replicated
- grad_w_out: float32 [128, 128], replicated
- grad_norm: float32 [4, 128], replicated
The draws below stay inside these ranges and needn't reach their ends.
All inputs are finite; a program needn't handle non-finite values.
Results may differ from the reference program's by a relative error of at most 0.012.
Values may be sent and summed in bfloat16 or wider, within the bound.
No kernel may reach another device: no remote copies, remote signals or barrier semaphores. Data moves between devices by JAX's collectives and lax.ppermute only.
A program may use at most 64 MiB of HBM per device.

```python
import jax
import jax.numpy as jnp
from jax import lax

C = 128
CH = 128
TILE = 24
N = 384
N_ROW = 16


def steps_of(own_key, shape, cuts, smallest, largest):
    level = 1.0
    for position, shards_of in cuts:
        heights = jax.random.uniform(jax.random.fold_in(jax.random.fold_in(own_key, 6), position), (shards_of,), jnp.float32, smallest / len(cuts), largest / len(cuts))
        level = level * jnp.repeat(jnp.exp(heights), shape[position] // shards_of).reshape((-1,) + (1,) * (len(shape) - 1 - position))
    return level


def centred(stream_key, shape, deviation, most, shards=(), kind=jnp.bfloat16):
    factor_of = steps_of(stream_key, shape, shards, -0.22, 0.18) if shards else 1.0
    drawn = jax.random.normal(stream_key, shape, jnp.float32) * deviation * factor_of
    return jnp.minimum(jnp.maximum(drawn, -most), most).astype(kind)


def setup_inputs(seed: int = 0) -> dict:
    splits = jax.random.split(jax.random.key(seed), 6)
    return {
        "pair": centred(splits[0], (N, N, C), 1.0, 6.0, ((0, 16), (1, 16))),
        "cotangent": centred(splits[1], (N, N, C), 1.0, 6.0, ((0, 16), (1, 16))),
        "w_in": centred(splits[2], (C, 5 * CH), C ** -0.5, 0.5),
        "w_out": centred(splits[3], (CH, C), CH ** -0.5, 0.5),
        "norm_params": jnp.clip(1.0 + 0.18 * jax.random.normal(splits[4], (4, C), jnp.float32), 0.1, 1.9),
    }


def norm_fwd(v, gain, bias):
    mu = lax.optimization_barrier(jnp.mean(v, axis=-1, keepdims=True))
    var = lax.optimization_barrier(jnp.mean((v - mu) ** 2, axis=-1, keepdims=True))
    rstd = 1.0 / jnp.sqrt(var + 1e-05)
    hat = (v - mu) * rstd
    return (hat * gain + bias, hat, rstd)

def norm_back(dout, hat, rstd, gain):
    inner = dout * gain
    return rstd * (inner - lax.optimization_barrier(jnp.mean(inner, axis=-1, keepdims=True)) - hat * lax.optimization_barrier(jnp.mean(inner * hat, axis=-1, keepdims=True)))

def reference(pair, cotangent, w_in, w_out, norm_params):
    f32 = jnp.float32
    zn_f, hat0, rstd0 = norm_fwd(pair.astype(f32), norm_params[0], norm_params[1])
    zn = zn_f.astype(jnp.bfloat16)
    proj = jnp.einsum('ijc,cd->ijd', zn.astype(f32), w_in.astype(f32))
    p0, p1, p2, p3, p4 = [proj[..., m * CH:(m + 1) * CH] for m in range(5)]
    s1 = jax.nn.sigmoid(p1)
    s3 = jax.nn.sigmoid(p3)
    gate = jax.nn.sigmoid(p4)
    a_val = (s1 * p0).astype(jnp.bfloat16)
    b_val = (s3 * p2).astype(jnp.bfloat16)
    x = jnp.einsum('ikc,jkc->ijc', a_val.astype(f32), b_val.astype(f32))
    xn_f, hat2, rstd2 = norm_fwd(x, norm_params[2], norm_params[3])
    xn = xn_f.astype(jnp.bfloat16)
    y = jnp.einsum('ijc,cd->ijd', xn.astype(f32), w_out.astype(f32))
    update = (gate * y).astype(jnp.bfloat16)
    dout = cotangent.astype(f32)
    dy = (dout * gate).astype(jnp.bfloat16)
    dp4 = dout * y * gate * (1.0 - gate)
    grad_w_out = jnp.einsum('ijc,ijd->cd', xn.astype(f32), dy.astype(f32)) / N
    dxn = jnp.einsum('ijd,cd->ijc', dy.astype(f32), w_out.astype(f32))
    dx = norm_back(dxn, hat2, rstd2, norm_params[2]).astype(jnp.bfloat16)
    da = jnp.einsum('ijc,jkc->ikc', dx.astype(f32), b_val.astype(f32))
    dx_blocks = dx.reshape(N_ROW, TILE, N, C)
    a_blocks = a_val.reshape(N_ROW, TILE, N, C)

    def add_block(total, pieces):
        dx_piece, a_piece = pieces
        partial_value = jnp.einsum('ijc,ikc->jkc', dx_piece.astype(f32), a_piece.astype(f32))
        return (total + partial_value.astype(jnp.bfloat16).astype(f32), None)
    db, _ = lax.scan(add_block, jnp.zeros((N, N, C), f32), (dx_blocks, a_blocks))
    d_all = jnp.concatenate([da * s1, da * p0 * s1 * (1.0 - s1), db * s3, db * p2 * s3 * (1.0 - s3), dp4], axis=-1).astype(jnp.bfloat16)
    grad_w_in = jnp.einsum('ijc,ijd->cd', zn.astype(f32), d_all.astype(f32)) / N
    dzn = jnp.einsum('ijd,cd->ijc', d_all.astype(f32), w_in.astype(f32))
    grad_pair = norm_back(dzn, hat0, rstd0, norm_params[0]).astype(jnp.bfloat16)
    grad_norm = jnp.stack([lax.optimization_barrier(jnp.sum(dzn * hat0, axis=(0, 1))), lax.optimization_barrier(jnp.sum(dzn, axis=(0, 1))), lax.optimization_barrier(jnp.sum(dxn * hat2, axis=(0, 1))), lax.optimization_barrier(jnp.sum(dxn, axis=(0, 1)))]) / N
    return (update, grad_pair, grad_w_in, grad_w_out, grad_norm)
```

```python
import jax
import jax.numpy as jnp
from jax import lax
from jax.experimental import pallas as pl
from jax.experimental.pallas import tpu as pltpu
from jax.sharding import Mesh
from jax.sharding import PartitionSpec as P

F32 = jnp.float32
BF16 = jnp.bfloat16
EPS = 1e-05
ROWS = 16
COLS = 8
CHIPS = 128
TILE = 24
WIDE = 32
TROWS = 6
POS = TILE * WIDE
C = 128


def dot(x, y, cx, cy):
    return lax.dot_general(x, y, (((cx,), (cy,)), ((), ())), preferred_element_type=F32)


def block_turn(parts):
    lane = lax.broadcasted_iota(jnp.int32, parts[0].shape, 1)
    for bit, shift in ((1, 32), (2, 64)):
        low = (lane & shift) == 0
        out = [None] * 4
        for i in range(4):
            if i & bit:
                continue
            x, y = parts[i], parts[i | bit]
            out[i] = jnp.where(low, x, pltpu.roll(y, shift, 1))
            out[i | bit] = jnp.where(low, pltpu.roll(x, 128 - shift, 1), y)
        parts = out
    return parts


def norm_lanes(v):
    mu = jnp.mean(v, axis=-1, keepdims=True)
    d = v - mu
    rstd = 1.0 / jnp.sqrt(jnp.mean(d * d, axis=-1, keepdims=True) + EPS)
    return d * rstd, rstd


def padded(tile):
    wide = jnp.concatenate([tile.astype(F32), jnp.zeros((TILE, WIDE - TILE, C), F32)], axis=1)
    return wide.reshape(POS, C)


def zero_rows(scr, rows, used):
    for t in range(used, rows):
        scr[pl.ds(t, CHIPS, stride=rows), :] = jnp.zeros((CHIPS, 128), F32)


def first_kernel(pair_ref, w_ref, norm_ref, send_ref, zn_ref, scr):
    hat, _ = norm_lanes(pair_ref[...].astype(F32))
    zn = padded(hat * norm_ref[0:1, :][None] + norm_ref[1:2, :][None]).astype(BF16)
    zn_ref[...] = zn
    for m in range(2):
        w = w_ref[:, 2 * m * C : (2 * m + 2) * C]
        p = dot(w, zn, 0, 1)
        val = jax.nn.sigmoid(p[C:]) * p[:C]
        for t in range(TROWS):
            scr[pl.ds(TROWS * m + t, CHIPS, stride=16), :] = val[:, t * 128 : (t + 1) * 128]
    zero_rows(scr, 16, 2 * TROWS)
    send_ref[...] = scr[...].astype(BF16).reshape(CHIPS, 16, 128)


def gather_rows(scr, rows, offset, dst):
    for g in range(2):
        for t in range(TROWS):
            parts = [scr[pl.ds((4 * g + u) * rows + offset + t, ROWS, stride=COLS * rows), :] for u in range(4)]
            for v, o in enumerate(block_turn(parts)):
                dst[pl.ds(16 * (4 * t + v), 16), g * 128 : (g + 1) * 128] = o.astype(BF16)


def scatter_rows(val, scr, rows, offset):
    for g in range(2):
        for t in range(TROWS):
            parts = [val[16 * (4 * t + v) : 16 * (4 * t + v) + 16, g * 128 : (g + 1) * 128] for v in range(4)]
            for u, o in enumerate(block_turn(parts)):
                scr[pl.ds((4 * g + u) * rows + offset + t, ROWS, stride=COLS * rows), :] = o


def second_kernel(core_ref, own_ref, sib_ref, send_ref, a_ref, b_ref, scr, a_sib, bscr, b_sib, sscr):
    core = core_ref[0]
    total = None
    for src, a_dst, b_dst in ((own_ref, a_ref, b_ref), (sib_ref, a_sib, b_sib)):
        scr[...] = src[...].astype(F32).reshape(CHIPS * 16, 128)
        gather_rows(scr, 16, 0, a_dst)
        bscr[...] = jnp.zeros(bscr.shape, F32)
        for g in range(2):
            for t in range(TROWS):
                parts = [scr[pl.ds((4 * g + u) * 16 + TROWS + t, ROWS, stride=COLS * 16), :] for u in range(4)]
                for v, o in enumerate(block_turn(parts)):
                    bscr[pl.ds(512 * g + 4 * t + v, ROWS, stride=WIDE), :] = o
        for g in range(2):
            b_dst[:, :, :, g * 128 : (g + 1) * 128] = bscr[512 * g : 512 * g + 512, :].astype(BF16).reshape(COLS, 2, WIDE, 128)
        part = dot(a_dst[...], b_dst[:, core].reshape(COLS * WIDE, 256), 1, 1)
        total = part if total is None else total + part
    scatter_rows(total, sscr, 8, 0)
    zero_rows(sscr, 8, TROWS)
    send_ref[...] = sscr[...].astype(BF16).reshape(CHIPS, 8, 128)


def column(row):
    return jnp.broadcast_to(row, (C, C)).T[:, :1]


def lane_sums(val):
    part = val[:, :128]
    for t in range(1, TROWS):
        part = part + val[:, t * 128 : (t + 1) * 128]
    return jnp.sum(part.T, axis=0, keepdims=True)


def third_kernel(recv_ref, zn_ref, cot_ref, w4_ref, wo_ref, norm_ref, send_ref, upd_ref, dp4_ref, gwo_ref, mid_ref, scr):
    scr[...] = recv_ref[...].astype(F32).reshape(CHIPS * 8, 128)
    x = jnp.concatenate([scr[pl.ds(t, CHIPS, stride=8), :] for t in range(TROWS)], axis=1)
    gain, bias = column(norm_ref[2:3, :]), column(norm_ref[3:4, :])
    mu = jnp.mean(x, axis=0, keepdims=True)
    d = x - mu
    rstd = 1.0 / jnp.sqrt(jnp.mean(d * d, axis=0, keepdims=True) + EPS)
    hat = d * rstd
    xn = (hat * gain + bias).astype(BF16)
    y = dot(wo_ref[...], xn, 0, 0)
    gate = jax.nn.sigmoid(dot(w4_ref[...], zn_ref[...], 0, 1))
    upd = (gate * y).T.reshape(TILE, WIDE, C)[:, :TILE, :]
    upd_ref[...] = upd.astype(BF16)
    cot = padded(cot_ref[...]).T
    cg = cot * gate
    dy = cg.astype(BF16)
    dp4_ref[...] = (cg * y * (1.0 - gate)).astype(BF16)
    gwo_ref[...] = dot(xn, dy, 1, 1)
    dxn = dot(wo_ref[...], dy, 1, 0)
    mid_ref[0:1, :] = lane_sums(dxn * hat)
    mid_ref[1:2, :] = lane_sums(dxn)
    mid_ref[2:8, :] = jnp.zeros((6, 128), F32)
    e = dxn * gain
    dx = rstd * (e - jnp.mean(e, axis=0, keepdims=True) - hat * jnp.mean(e * hat, axis=0, keepdims=True))
    for t in range(TROWS):
        scr[pl.ds(t, CHIPS, stride=8), :] = dx[:, t * 128 : (t + 1) * 128]
    zero_rows(scr, 8, TROWS)
    send_ref[...] = scr[...].astype(BF16).reshape(CHIPS, 8, 128)


def fourth_kernel(core_ref, own_ref, sib_ref, a_ref, b_ref, send_ref, scr, d_ref, dbscr, sscr):
    core = core_ref[0]
    da = None
    for src, side in ((own_ref, core), (sib_ref, 1 - core)):
        scr[...] = src[...].astype(F32).reshape(CHIPS * 8, 128)
        gather_rows(scr, 8, 0, d_ref)
        dx = d_ref[...]
        part = dot(dx, b_ref[:, side].reshape(COLS * WIDE, 256), 1, 0)
        da = part if da is None else da + part
        db = dot(dx, a_ref[...], 0, 0)
        for g in range(2):
            dbscr[pl.ds(256 * g, 256), :] = db[:, g * 128 : (g + 1) * 128]
        for g in range(2):
            for t in range(TROWS):
                parts = [dbscr[pl.ds(256 * g + 4 * t + v, COLS, stride=WIDE), :] for v in range(4)]
                for u, o in enumerate(block_turn(parts)):
                    sscr[pl.ds(side * 128 + (4 * g + u) * 16 + TROWS + t, COLS, stride=256), :] = o
    scatter_rows(da, sscr, 16, 0)
    zero_rows(sscr, 16, 2 * TROWS)
    send_ref[...] = sscr[...].astype(BF16).reshape(CHIPS, 16, 128)


def fifth_kernel(recv_ref, zn_ref, pair_ref, w_ref, dp4_ref, gwo_ref, mid_ref, norm_ref, gpair_ref, g_ref, scr):
    scr[...] = recv_ref[...].astype(F32).reshape(CHIPS * 16, 128)
    zn = zn_ref[...]
    blocks = []
    for m in range(2):
        grad = jnp.concatenate([scr[pl.ds(TROWS * m + t, CHIPS, stride=16), :] for t in range(TROWS)], axis=1)
        p = dot(w_ref[:, 2 * m * C : (2 * m + 2) * C], zn, 0, 1)
        s = jax.nn.sigmoid(p[C:])
        gs = grad * s
        blocks += [gs.astype(BF16), (gs * p[:C] * (1.0 - s)).astype(BF16)]
    dp = jnp.concatenate(blocks + [dp4_ref[...]], axis=0)
    g_ref[0 : 5 * C, :] = dot(dp, zn, 1, 0)
    g_ref[5 * C : 6 * C, :] = gwo_ref[...]
    dzn = dot(w_ref[...], dp, 1, 0).T
    hat, rstd = norm_lanes(padded(pair_ref[...]))
    e = dzn * norm_ref[0:1, :]
    back = rstd * (e - jnp.mean(e, axis=-1, keepdims=True) - hat * jnp.mean(e * hat, axis=-1, keepdims=True))
    gpair_ref[...] = back.reshape(TILE, WIDE, C)[:, :TILE, :].astype(BF16)
    g_ref[6 * C : 6 * C + 8, :] = mid_ref[...]
    g_ref[6 * C + 2 : 6 * C + 3, :] = jnp.sum(dzn * hat, axis=0, keepdims=True)
    g_ref[6 * C + 3 : 6 * C + 4, :] = jnp.sum(dzn, axis=0, keepdims=True)
    g_ref[6 * C + 8 : 8 * C, :] = jnp.zeros((2 * C - 8, 128), F32)


def call(kernel, outs, scratch, *args, scalars=0):
    vmem = pl.BlockSpec(memory_space=pltpu.VMEM)
    smem = pl.BlockSpec(memory_space=pltpu.SMEM)
    return pl.pallas_call(
        kernel,
        out_shape=[jax.ShapeDtypeStruct(s, t) for s, t in outs],
        in_specs=[smem] * scalars + [vmem] * (len(args) - scalars),
        out_specs=[vmem] * len(outs),
        scratch_shapes=[pltpu.VMEM(s, t) for s, t in scratch],
        compiler_params=pltpu.CompilerParams(vmem_limit_bytes=40 * 1024 * 1024),
    )(*args)


def shards(pair, cotangent, w_in, w_out, norm_params):
    chips = ("row", "q")
    swap = [(0, 1), (1, 0)]

    def turn(x):
        return lax.all_to_all(x, chips, split_axis=0, concat_axis=0, tiled=True)

    core = lax.axis_index("core").astype(jnp.int32).reshape(1)
    send, zn = call(
        first_kernel, [((CHIPS, 16, 128), BF16), ((POS, C), BF16)], [((CHIPS * 16, 128), F32)], pair, w_in, norm_params
    )
    own = turn(send)
    sib = lax.ppermute(own, "core", swap)
    send, a_own, b_own = call(
        second_kernel,
        [((CHIPS, 8, 128), BF16), ((384, 256), BF16), ((COLS, 2, WIDE, 256), BF16)],
        [
            ((CHIPS * 16, 128), F32),
            ((384, 256), BF16),
            ((1024, 128), F32),
            ((COLS, 2, WIDE, 256), BF16),
            ((CHIPS * 8, 128), F32),
        ],
        core,
        own,
        sib,
        scalars=1,
    )
    recv = turn(send)
    send, update, dp4, gwo, mid = call(
        third_kernel,
        [
            ((CHIPS, 8, 128), BF16),
            ((TILE, TILE, C), BF16),
            ((C, POS), BF16),
            ((C, C), F32),
            ((8, 128), F32),
        ],
        [((CHIPS * 8, 128), F32)],
        recv,
        zn,
        cotangent,
        w_in[:, 4 * C :],
        w_out,
        norm_params,
    )
    own = turn(send)
    sib = lax.ppermute(own, "core", swap)
    (send,) = call(
        fourth_kernel,
        [((CHIPS, 16, 128), BF16)],
        [((CHIPS * 8, 128), F32), ((384, 256), BF16), ((512, 128), F32), ((CHIPS * 16, 128), F32)],
        core,
        own,
        sib,
        a_own,
        b_own,
        scalars=1,
    )
    recv = turn(send)
    grad_pair, grads = call(
        fifth_kernel,
        [((TILE, TILE, C), BF16), ((8 * C, 128), F32)],
        [((CHIPS * 16, 128), F32)],
        recv,
        zn,
        pair,
        w_in,
        dp4,
        gwo,
        mid,
        norm_params,
    )
    mine = jnp.sum(turn(grads.reshape(CHIPS, 8, 128)), axis=0)
    mine = (mine + lax.ppermute(mine, "core", swap)) / 384.0
    full = turn(jnp.broadcast_to(mine[None], (CHIPS, 8, 128))).reshape(8 * C, 128)
    grad_w_in = full[: 5 * C].T
    grad_w_out = full[5 * C : 6 * C]
    norms = full[6 * C : 6 * C + 4]
    grad_norm = jnp.concatenate([norms[2:4], norms[0:2]], axis=0)
    return (update, grad_pair, grad_w_in, grad_w_out, grad_norm)


def solution(mesh):
    fine = Mesh(mesh.devices.reshape(ROWS, COLS, 2), ("row", "q", "core"))
    placed = (P("row", ("q", "core"), None), P("row", ("q", "core"), None), P(), P(), P())
    return jax.shard_map(shards, mesh=fine, in_specs=placed, out_specs=placed, check_vma=False)
```

```python
import jax
import jax.numpy as jnp
from jax import lax
from jax.experimental import pallas as pl
from jax.experimental.pallas import tpu as pltpu
from jax.sharding import Mesh
from jax.sharding import PartitionSpec as P

F32 = jnp.float32
BF16 = jnp.bfloat16
EPS = 1e-05
ROWS = 16
COLS = 8
CHIPS = 128
TILE = 24
WIDE = 32
TROWS = 6
POS = TILE * WIDE
C = 128


def dot(x, y, cx, cy):
    return lax.dot_general(x, y, (((cx,), (cy,)), ((), ())), preferred_element_type=F32)


def block_turn(parts):
    lane = lax.broadcasted_iota(jnp.int32, parts[0].shape, 1)
    for bit, shift in ((1, 32), (2, 64)):
        low = (lane & shift) == 0
        out = [None] * 4
        for i in range(4):
            if i & bit:
                continue
            x, y = parts[i], parts[i | bit]
            out[i] = jnp.where(low, x, pltpu.roll(y, shift, 1))
            out[i | bit] = jnp.where(low, pltpu.roll(x, 128 - shift, 1), y)
        parts = out
    return parts


def norm_lanes(v):
    mu = jnp.mean(v, axis=-1, keepdims=True)
    d = v - mu
    rstd = 1.0 / jnp.sqrt(jnp.mean(d * d, axis=-1, keepdims=True) + EPS)
    return d * rstd, rstd


def padded(tile):
    wide = jnp.concatenate([tile.astype(F32), jnp.zeros((TILE, WIDE - TILE, C), F32)], axis=1)
    return wide.reshape(POS, C)


def first_kernel(pair_hbm, w_hbm, norm_hbm, send_ref, zn_ref, pair_ref, w_ref, norm_ref, sems):
    copies = [
        pltpu.make_async_copy(src, dst, sems.at[i])
        for i, (src, dst) in enumerate(((pair_hbm, pair_ref), (norm_hbm, norm_ref), (w_hbm, w_ref)))
    ]
    for copy in copies:
        copy.start()
    copies[0].wait()
    hat, _ = norm_lanes(pair_ref[...].astype(F32))
    copies[1].wait()
    zn = padded(hat * norm_ref[0:1, :][None] + norm_ref[1:2, :][None]).astype(BF16)
    zn_ref[...] = zn
    copies[2].wait()
    for m in range(2):
        p = dot(w_ref[:, 2 * m * C : (2 * m + 2) * C], zn, 0, 1)
        send_ref[:, m, :] = (jax.nn.sigmoid(p[C:]) * p[:C]).astype(BF16)


def unpack(src, row, t0, scr):
    for t in range(src.shape[2] // 128):
        scr[pl.ds((t0 + t) * CHIPS, CHIPS), :] = src[:, row, t * 128 : (t + 1) * 128].astype(F32)


def gather_rows(scr, t0, dst):
    for g in range(2):
        for t in range(TROWS):
            parts = [scr[pl.ds((t0 + t) * CHIPS + 4 * g + u, ROWS, stride=COLS), :] for u in range(4)]
            for v, o in enumerate(block_turn(parts)):
                dst[pl.ds(16 * (4 * t + v), 16), g * 128 : (g + 1) * 128] = o.astype(BF16)


def scatter_rows(val, scr, t0):
    for g in range(2):
        for t in range(TROWS):
            parts = [val[16 * (4 * t + v) : 16 * (4 * t + v) + 16, g * 128 : (g + 1) * 128] for v in range(4)]
            for u, o in enumerate(block_turn(parts)):
                scr[pl.ds((t0 + t) * CHIPS + 4 * g + u, ROWS, stride=COLS), :] = o


def product(core, src, a_dst, b_dst, scr, bscr):
    unpack(src, 0, 0, scr)
    unpack(src, 1, TROWS, scr)
    gather_rows(scr, 0, a_dst)
    for half in range(2 * 16):
        bscr[pl.ds(half * WIDE + TILE, WIDE - TILE), :] = jnp.zeros((WIDE - TILE, 128), F32)
    for g in range(2):
        for t in range(TROWS):
            parts = [scr[pl.ds((TROWS + t) * CHIPS + 4 * g + u, ROWS, stride=COLS), :] for u in range(4)]
            for v, o in enumerate(block_turn(parts)):
                bscr[pl.ds(512 * g + 4 * t + v, ROWS, stride=WIDE), :] = o
    for g in range(2):
        b_dst[:, :, :, g * 128 : (g + 1) * 128] = bscr[512 * g : 512 * g + 512, :].astype(BF16).reshape(COLS, 2, WIDE, 128)
    return dot(a_dst[...], b_dst[:, core].reshape(COLS * WIDE, 256), 1, 1)


def second_kernel(core_ref, src_ref, part_ref, a_ref, b_ref, scr, bscr):
    part_ref[...] = product(core_ref[0], src_ref, a_ref, b_ref, scr, bscr)


def second_kernel_sib(core_ref, src_ref, part_ref, send_ref, scr, bscr, a_ref, b_ref):
    total = part_ref[...] + product(core_ref[0], src_ref, a_ref, b_ref, scr, bscr)
    scatter_rows(total, scr, 0)
    pack(scr, 0, send_ref, 384)


def pack(scr, t0, dst, width):
    per = width // 128
    for s in range(2):
        for t in range(per):
            dst[:, s, t * 128 : (t + 1) * 128] = scr[pl.ds((t0 + s * per + t) * CHIPS, CHIPS), :].astype(BF16)


def column(row):
    return jnp.broadcast_to(row, (C, C)).T[:, :1]


def lane_sums(val):
    part = val[:, :128]
    for t in range(1, TROWS):
        part = part + val[:, t * 128 : (t + 1) * 128]
    return jnp.sum(part.T, axis=0, keepdims=True)


def third_kernel(recv_ref, zn_ref, cot_ref, w_ref, wo_ref, norm_ref, send_ref, upd_ref, dp4_ref, gwo_ref, mid_ref):
    x = jnp.concatenate([recv_ref[:, s, :].astype(F32) for s in range(2)], axis=1)
    gain, bias = column(norm_ref[2:3, :]), column(norm_ref[3:4, :])
    mu = jnp.mean(x, axis=0, keepdims=True)
    d = x - mu
    rstd = 1.0 / jnp.sqrt(jnp.mean(d * d, axis=0, keepdims=True) + EPS)
    hat = d * rstd
    xn = (hat * gain + bias).astype(BF16)
    y = dot(wo_ref[...], xn, 0, 0)
    gate = jax.nn.sigmoid(dot(w_ref[:, 4 * C :], zn_ref[...], 0, 1))
    upd = (gate * y).T.reshape(TILE, WIDE, C)[:, :TILE, :]
    upd_ref[...] = upd.astype(BF16)
    cot = padded(cot_ref[...]).T
    cg = cot * gate
    dy = cg.astype(BF16)
    dp4_ref[...] = (cg * y * (1.0 - gate)).astype(BF16)
    gwo_ref[...] = dot(xn, dy, 1, 1)
    dxn = dot(wo_ref[...], dy, 1, 0)
    mid_ref[0:1, :] = lane_sums(dxn * hat)
    mid_ref[1:2, :] = lane_sums(dxn)
    mid_ref[2:8, :] = jnp.zeros((6, 128), F32)
    e = dxn * gain
    dx = rstd * (e - jnp.mean(e, axis=0, keepdims=True) - hat * jnp.mean(e * hat, axis=0, keepdims=True))
    for half in range(2):
        send_ref[:, half, :] = dx[:, half * 384 : (half + 1) * 384].astype(BF16)


def back_product(side, src, a_ref, b_ref, scr, d_ref, dbscr, sscr):
    unpack(src, 0, 0, scr)
    unpack(src, 1, 3, scr)
    gather_rows(scr, 0, d_ref)
    dx = d_ref[...]
    db = dot(dx, a_ref[...], 0, 0)
    for g in range(2):
        dbscr[pl.ds(256 * g, 256), :] = db[:, g * 128 : (g + 1) * 128]
    for g in range(2):
        for t in range(TROWS):
            parts = [dbscr[pl.ds(256 * g + 4 * t + v, COLS, stride=WIDE), :] for v in range(4)]
            for u, o in enumerate(block_turn(parts)):
                sscr[pl.ds(t * CHIPS + 8 * side + 4 * g + u, COLS, stride=16), :] = o
    return dot(dx, b_ref[:, side].reshape(COLS * WIDE, 256), 1, 0)


def fourth_kernel(core_ref, src_ref, a_ref, b_ref, da_ref, db_ref, scr, d_ref, dbscr):
    da_ref[...] = back_product(core_ref[0], src_ref, a_ref, b_ref, scr, d_ref, dbscr, db_ref)


def fourth_kernel_sib(core_ref, src_ref, a_ref, b_ref, da_ref, db_ref, send_ref, scr, d_ref, dbscr, sscr):
    core = core_ref[0]
    da = da_ref[...] + back_product(1 - core, src_ref, a_ref, b_ref, scr, d_ref, dbscr, sscr)
    mine = (lax.broadcasted_iota(jnp.int32, (CHIPS, 128), 0) // COLS) % 2 == core
    for t in range(TROWS):
        tile = pl.ds(t * CHIPS, CHIPS)
        send_ref[:, 1, t * 128 : (t + 1) * 128] = jnp.where(mine, db_ref[tile, :], sscr[tile, :]).astype(BF16)
    scatter_rows(da, scr, 0)
    for t in range(TROWS):
        send_ref[:, 0, t * 128 : (t + 1) * 128] = scr[pl.ds(t * CHIPS, CHIPS), :].astype(BF16)


def fifth_kernel(recv_ref, zn_ref, pair_ref, w_ref, dp4_ref, gwo_ref, mid_ref, norm_ref, gpair_ref, g_ref):
    zn = zn_ref[...]
    blocks = []
    for m in range(2):
        grad = recv_ref[:, m, :].astype(F32)
        p = dot(w_ref[:, 2 * m * C : (2 * m + 2) * C], zn, 0, 1)
        s = jax.nn.sigmoid(p[C:])
        gs = grad * s
        blocks += [gs.astype(BF16), (gs * p[:C] * (1.0 - s)).astype(BF16)]
    dp = jnp.concatenate(blocks + [dp4_ref[...]], axis=0)
    g_ref[0 : 5 * C, :] = dot(dp, zn, 1, 0).astype(BF16)
    g_ref[5 * C : 6 * C, :] = gwo_ref[...].astype(BF16)
    dzn = dot(w_ref[...], dp, 1, 0).T
    hat, rstd = norm_lanes(padded(pair_ref[...]))
    e = dzn * norm_ref[0:1, :]
    back = rstd * (e - jnp.mean(e, axis=-1, keepdims=True) - hat * jnp.mean(e * hat, axis=-1, keepdims=True))
    gpair_ref[...] = back.reshape(TILE, WIDE, C)[:, :TILE, :].astype(BF16)
    first = jnp.sum(dzn * hat, axis=0, keepdims=True)
    second = jnp.sum(dzn, axis=0, keepdims=True)
    rows = jnp.concatenate([first, second, mid_ref[0:2, :], jnp.zeros((12, 128), F32)], axis=0)
    g_ref[6 * C : 6 * C + 16, :] = rows.astype(BF16)
    g_ref[6 * C + 16 : 8 * C, :] = jnp.zeros((2 * C - 16, 128), BF16)


def last_kernel(full_ref, gwi_ref, gwo_ref, gn_ref):
    for m in range(5):
        gwi_ref[:, m * C : (m + 1) * C] = full_ref[m * C : (m + 1) * C, :].astype(F32).T
    gwo_ref[...] = full_ref[5 * C : 6 * C, :].astype(F32)
    gn_ref[...] = full_ref[6 * C : 6 * C + 16, :].astype(F32)[0:4, :]


def call(kernel, outs, scratch, *args, scalars=0, anywhere=False):
    vmem = pl.BlockSpec(memory_space=pltpu.VMEM)
    smem = pl.BlockSpec(memory_space=pltpu.SMEM)
    rest = pl.BlockSpec(memory_space=pltpu.HBM) if anywhere else vmem
    return pl.pallas_call(
        kernel,
        out_shape=[jax.ShapeDtypeStruct(s, t) for s, t in outs],
        in_specs=[smem] * scalars + [rest] * (len(args) - scalars),
        out_specs=[vmem] * len(outs),
        scratch_shapes=scratch,
        compiler_params=pltpu.CompilerParams(vmem_limit_bytes=40 * 1024 * 1024),
    )(*args)


def shards(pair, cotangent, w_in, w_out, norm_params):
    chips = ("row", "q")
    swap = [(0, 1), (1, 0)]
    f32, bf16 = (lambda *s: pltpu.VMEM(s, F32)), (lambda *s: pltpu.VMEM(s, BF16))
    wide, thin = ((CHIPS, 2, 768), BF16), ((CHIPS, 2, 384), BF16)
    tiles = 2 * TROWS * CHIPS

    def turn(x):
        return lax.all_to_all(x, chips, split_axis=0, concat_axis=0, tiled=True)

    core = lax.axis_index("core").astype(jnp.int32).reshape(1)
    send, zn = call(
        first_kernel,
        [wide, ((POS, C), BF16)],
        [bf16(TILE, TILE, C), bf16(C, 5 * C), f32(4, C), pltpu.SemaphoreType.DMA((3,))],
        pair,
        w_in,
        norm_params,
        anywhere=True,
    )
    own = turn(send)
    sib = lax.ppermute(own, "core", swap)
    part, a_own, b_own = call(
        second_kernel,
        [((384, 256), F32), ((384, 256), BF16), ((COLS, 2, WIDE, 256), BF16)],
        [f32(tiles, 128), f32(1024, 128)],
        core,
        own,
        scalars=1,
    )
    (send,) = call(
        second_kernel_sib,
        [thin],
        [f32(tiles, 128), f32(1024, 128), bf16(384, 256), bf16(COLS, 2, WIDE, 256)],
        core,
        sib,
        part,
        scalars=1,
    )
    send, update, dp4, gwo, mid = call(
        third_kernel,
        [thin, ((TILE, TILE, C), BF16), ((C, POS), BF16), ((C, C), F32), ((8, 128), F32)],
        [],
        turn(send),
        zn,
        cotangent,
        w_in,
        w_out,
        norm_params,
    )
    own = turn(send)
    sib = lax.ppermute(own, "core", swap)
    scratch = [f32(tiles // 2, 128), bf16(384, 256), f32(512, 128)]
    da, db = call(
        fourth_kernel,
        [((384, 256), F32), ((tiles // 2, 128), F32)],
        scratch,
        core,
        own,
        a_own,
        b_own,
        scalars=1,
    )
    (send,) = call(
        fourth_kernel_sib, [wide], scratch + [f32(tiles // 2, 128)], core, sib, a_own, b_own, da, db, scalars=1
    )
    grad_pair, grads = call(
        fifth_kernel,
        [((TILE, TILE, C), BF16), ((8 * C, 128), BF16)],
        [],
        turn(send),
        zn,
        pair,
        w_in,
        dp4,
        gwo,
        mid,
        norm_params,
    )
    mine = jnp.sum(turn(grads.reshape(CHIPS, 8, 128)).astype(F32), axis=0)
    mine = ((mine + lax.ppermute(mine, "core", swap)) / 384.0).astype(BF16)
    full = turn(jnp.broadcast_to(mine[None], (CHIPS, 8, 128))).reshape(8 * C, 128)
    grad_w_in, grad_w_out, grad_norm = call(
        last_kernel, [((C, 5 * C), F32), ((C, C), F32), ((4, C), F32)], [], full
    )
    return (update, grad_pair, grad_w_in, grad_w_out, grad_norm)


def solution(mesh):
    fine = Mesh(mesh.devices.reshape(ROWS, COLS, 2), ("row", "q", "core"))
    placed = (P("row", ("q", "core"), None), P("row", ("q", "core"), None), P(), P(), P())
    return jax.shard_map(shards, mesh=fine, in_specs=placed, out_specs=placed, check_vma=False)
```

```python
import functools

import jax
import jax.numpy as jnp
from jax import lax
from jax.experimental import pallas as pl
from jax.experimental.pallas import tpu as pltpu
from jax.sharding import Mesh
from jax.sharding import PartitionSpec as P

F32 = jnp.float32
BF16 = jnp.bfloat16
EPS = 1e-05
ROWS = 16
COLS = 8
CHIPS = 128
TILE = 24
WIDE = 32
TROWS = 6
POS = TILE * WIDE
C = 128
PLANE = 32
CHIP_AXES = ("z", "yl", "x", "yh")
PLANE_AXES = ("yl", "x", "yh", "core")


def dot(x, y, cx, cy):
    return lax.dot_general(x, y, (((cx,), (cy,)), ((), ())), preferred_element_type=F32)


def block_turn(parts):
    lane = lax.broadcasted_iota(jnp.int32, parts[0].shape, 1)
    for bit, shift in ((1, 32), (2, 64)):
        low = (lane & shift) == 0
        out = [None] * 4
        for i in range(4):
            if i & bit:
                continue
            x, y = parts[i], parts[i | bit]
            out[i] = jnp.where(low, x, pltpu.roll(y, shift, 1))
            out[i | bit] = jnp.where(low, pltpu.roll(x, 128 - shift, 1), y)
        parts = out
    return parts


def norm_lanes(v):
    mu = jnp.mean(v, axis=-1, keepdims=True)
    d = v - mu
    rstd = 1.0 / jnp.sqrt(jnp.mean(d * d, axis=-1, keepdims=True) + EPS)
    return d * rstd, rstd


def padded(tile):
    wide = jnp.concatenate([tile.astype(F32), jnp.zeros((TILE, WIDE - TILE, C), F32)], axis=1)
    return wide.reshape(POS, C)


def first_kernel(pair_hbm, w_hbm, norm_hbm, send_ref, zn_ref, pair_ref, w_ref, norm_ref, sems):
    copies = [
        pltpu.make_async_copy(src, dst, sems.at[i])
        for i, (src, dst) in enumerate(((pair_hbm, pair_ref), (norm_hbm, norm_ref), (w_hbm, w_ref)))
    ]
    for copy in copies:
        copy.start()
    copies[0].wait()
    hat, _ = norm_lanes(pair_ref[...].astype(F32))
    copies[1].wait()
    zn = padded(hat * norm_ref[0:1, :][None] + norm_ref[1:2, :][None]).astype(BF16)
    zn_ref[...] = zn
    copies[2].wait()
    for m in range(2):
        p = dot(w_ref[:, 2 * m * C : (2 * m + 2) * C], zn, 0, 1)
        send_ref[:, m, :] = (jax.nn.sigmoid(p[C:]) * p[:C]).astype(BF16)


def unpack(src, row, t0, scr):
    for t in range(src.shape[2] // 128):
        scr[pl.ds((t0 + t) * CHIPS, CHIPS), :] = src[:, row, t * 128 : (t + 1) * 128].astype(F32)


def gather_rows(scr, t0, dst):
    for g in range(2):
        for t in range(TROWS):
            parts = [scr[pl.ds((t0 + t) * CHIPS + 4 * g + u, ROWS, stride=COLS), :] for u in range(4)]
            for v, o in enumerate(block_turn(parts)):
                dst[pl.ds(16 * (4 * t + v), 16), g * 128 : (g + 1) * 128] = o.astype(BF16)


def scatter_rows(val, scr, t0):
    for g in range(2):
        for t in range(TROWS):
            parts = [val[16 * (4 * t + v) : 16 * (4 * t + v) + 16, g * 128 : (g + 1) * 128] for v in range(4)]
            for u, o in enumerate(block_turn(parts)):
                scr[pl.ds((t0 + t) * CHIPS + 4 * g + u, ROWS, stride=COLS), :] = o


def product(core, src, a_dst, b_dst, scr, bscr):
    unpack(src, 0, 0, scr)
    unpack(src, 1, TROWS, scr)
    gather_rows(scr, 0, a_dst)
    for half in range(2 * 16):
        bscr[pl.ds(half * WIDE + TILE, WIDE - TILE), :] = jnp.zeros((WIDE - TILE, 128), F32)
    for g in range(2):
        for t in range(TROWS):
            parts = [scr[pl.ds((TROWS + t) * CHIPS + 4 * g + u, ROWS, stride=COLS), :] for u in range(4)]
            for v, o in enumerate(block_turn(parts)):
                bscr[pl.ds(512 * g + 4 * t + v, ROWS, stride=WIDE), :] = o
    for g in range(2):
        b_dst[:, :, :, g * 128 : (g + 1) * 128] = bscr[512 * g : 512 * g + 512, :].astype(BF16).reshape(COLS, 2, WIDE, 128)
    return dot(a_dst[...], b_dst[:, core].reshape(COLS * WIDE, 256), 1, 1)


def second_kernel(core_ref, src_ref, part_ref, a_ref, b_ref, scr, bscr):
    part_ref[...] = product(core_ref[0], src_ref, a_ref, b_ref, scr, bscr)


def second_kernel_sib(core_ref, src_ref, part_ref, send_ref, scr, bscr, a_ref, b_ref):
    total = part_ref[...] + product(core_ref[0], src_ref, a_ref, b_ref, scr, bscr)
    scatter_rows(total, scr, 0)
    pack(scr, 0, send_ref, 384)


def pack(scr, t0, dst, width):
    per = width // 128
    for s in range(2):
        for t in range(per):
            dst[:, s, t * 128 : (t + 1) * 128] = scr[pl.ds((t0 + s * per + t) * CHIPS, CHIPS), :].astype(BF16)


def column(row):
    return jnp.broadcast_to(row, (C, C)).T[:, :1]


def lane_sums(val):
    part = val[:, :128]
    for t in range(1, TROWS):
        part = part + val[:, t * 128 : (t + 1) * 128]
    return jnp.sum(part.T, axis=0, keepdims=True)


def third_kernel(recv_ref, zn_ref, cot_ref, w_ref, wo_ref, norm_ref, send_ref, upd_ref, dp4_ref, gwo_ref, mid_ref):
    x = jnp.concatenate([recv_ref[:, s, :].astype(F32) for s in range(2)], axis=1)
    gain, bias = column(norm_ref[2:3, :]), column(norm_ref[3:4, :])
    mu = jnp.mean(x, axis=0, keepdims=True)
    d = x - mu
    rstd = 1.0 / jnp.sqrt(jnp.mean(d * d, axis=0, keepdims=True) + EPS)
    hat = d * rstd
    xn = (hat * gain + bias).astype(BF16)
    y = dot(wo_ref[...], xn, 0, 0)
    gate = jax.nn.sigmoid(dot(w_ref[:, 4 * C :], zn_ref[...], 0, 1))
    upd = (gate * y).T.reshape(TILE, WIDE, C)[:, :TILE, :]
    upd_ref[...] = upd.astype(BF16)
    cot = padded(cot_ref[...]).T
    cg = cot * gate
    dy = cg.astype(BF16)
    dp4_ref[...] = (cg * y * (1.0 - gate)).astype(BF16)
    gwo_ref[...] = dot(xn, dy, 1, 1)
    dxn = dot(wo_ref[...], dy, 1, 0)
    mid_ref[0:1, :] = lane_sums(dxn * hat)
    mid_ref[1:2, :] = lane_sums(dxn)
    mid_ref[2:8, :] = jnp.zeros((6, 128), F32)
    e = dxn * gain
    dx = rstd * (e - jnp.mean(e, axis=0, keepdims=True) - hat * jnp.mean(e * hat, axis=0, keepdims=True))
    for half in range(2):
        send_ref[:, half, :] = dx[:, half * 384 : (half + 1) * 384].astype(BF16)


def back_product(side, src, a_ref, b_ref, scr, d_ref, dbscr, sscr):
    unpack(src, 0, 0, scr)
    unpack(src, 1, 3, scr)
    gather_rows(scr, 0, d_ref)
    dx = d_ref[...]
    db = dot(dx, a_ref[...], 0, 0)
    for g in range(2):
        dbscr[pl.ds(256 * g, 256), :] = db[:, g * 128 : (g + 1) * 128]
    for g in range(2):
        for t in range(TROWS):
            parts = [dbscr[pl.ds(256 * g + 4 * t + v, COLS, stride=WIDE), :] for v in range(4)]
            for u, o in enumerate(block_turn(parts)):
                sscr[pl.ds(t * CHIPS + 8 * side + 4 * g + u, COLS, stride=16), :] = o
    return dot(dx, b_ref[:, side].reshape(COLS * WIDE, 256), 1, 0)


def fourth_kernel(core_ref, src_ref, a_ref, b_ref, da_ref, db_ref, scr, d_ref, dbscr):
    da_ref[...] = back_product(core_ref[0], src_ref, a_ref, b_ref, scr, d_ref, dbscr, db_ref)


def fourth_kernel_sib(core_ref, src_ref, a_ref, b_ref, da_ref, db_ref, send_ref, scr, d_ref, dbscr, sscr):
    core = core_ref[0]
    da = da_ref[...] + back_product(1 - core, src_ref, a_ref, b_ref, scr, d_ref, dbscr, sscr)
    mine = (lax.broadcasted_iota(jnp.int32, (CHIPS, 128), 0) // COLS) % 2 == core
    for t in range(TROWS):
        tile = pl.ds(t * CHIPS, CHIPS)
        send_ref[:, 1, t * 128 : (t + 1) * 128] = jnp.where(mine, db_ref[tile, :], sscr[tile, :]).astype(BF16)
    scatter_rows(da, scr, 0)
    for t in range(TROWS):
        send_ref[:, 0, t * 128 : (t + 1) * 128] = scr[pl.ds(t * CHIPS, CHIPS), :].astype(BF16)


def fifth_kernel(recv_ref, zn_ref, pair_ref, w_ref, dp4_ref, gwo_ref, mid_ref, norm_ref, gpair_ref, g_ref):
    zn = zn_ref[...]
    blocks = []
    for m in range(2):
        grad = recv_ref[:, m, :].astype(F32)
        p = dot(w_ref[:, 2 * m * C : (2 * m + 2) * C], zn, 0, 1)
        s = jax.nn.sigmoid(p[C:])
        gs = grad * s
        blocks += [gs.astype(BF16), (gs * p[:C] * (1.0 - s)).astype(BF16)]
    dp = jnp.concatenate(blocks + [dp4_ref[...]], axis=0)
    dzn = dot(w_ref[...], dp, 1, 0).T
    hat, rstd = norm_lanes(padded(pair_ref[...]))
    e = dzn * norm_ref[0:1, :]
    back = rstd * (e - jnp.mean(e, axis=-1, keepdims=True) - hat * jnp.mean(e * hat, axis=-1, keepdims=True))
    gpair_ref[...] = back.reshape(TILE, WIDE, C)[:, :TILE, :].astype(BF16)
    first = jnp.sum(dzn * hat, axis=0, keepdims=True)
    second = jnp.sum(dzn, axis=0, keepdims=True)
    grads = jnp.concatenate([dot(dp, zn, 1, 0), gwo_ref[...]], axis=0).reshape(PLANE, 24, C)
    sums = jnp.concatenate([first, second, mid_ref[0:2, :], jnp.zeros((4, C), F32)], axis=0)[None]
    sums = jnp.concatenate([sums, jnp.zeros((PLANE - 1, 8, C), F32)], axis=0)
    g_ref[...] = jnp.concatenate([grads, sums], axis=1).astype(BF16)


def spread_kernel(recv_ref, send_ref, *, scale):
    total = jnp.sum(recv_ref[...].astype(F32), axis=0) * scale
    send_ref[...] = jnp.broadcast_to(total[None], send_ref.shape).astype(BF16)


def last_kernel(full_ref, gwi_ref, gwo_ref, gn_ref):
    full = full_ref[...].astype(F32)
    grads = full[:, :24, :].reshape(6 * C, C)
    for m in range(5):
        gwi_ref[:, m * C : (m + 1) * C] = grads[m * C : (m + 1) * C, :].T
    gwo_ref[...] = grads[5 * C :, :]
    gn_ref[...] = full[0, 24:28, :]


def call(kernel, outs, scratch, *args, scalars=0, anywhere=False):
    vmem = pl.BlockSpec(memory_space=pltpu.VMEM)
    smem = pl.BlockSpec(memory_space=pltpu.SMEM)
    rest = pl.BlockSpec(memory_space=pltpu.HBM) if anywhere else vmem
    return pl.pallas_call(
        kernel,
        out_shape=[jax.ShapeDtypeStruct(s, t) for s, t in outs],
        in_specs=[smem] * scalars + [rest] * (len(args) - scalars),
        out_specs=[vmem] * len(outs),
        scratch_shapes=scratch,
        compiler_params=pltpu.CompilerParams(vmem_limit_bytes=40 * 1024 * 1024),
    )(*args)


def shards(pair, cotangent, w_in, w_out, norm_params):
    swap = [(0, 1), (1, 0)]
    f32, bf16 = (lambda *s: pltpu.VMEM(s, F32)), (lambda *s: pltpu.VMEM(s, BF16))
    wide, thin = ((CHIPS, 2, 768), BF16), ((CHIPS, 2, 384), BF16)
    tiles = 2 * TROWS * CHIPS

    chunks = ((PLANE, 32, C), BF16)

    def turn(x, axes=CHIP_AXES):
        return lax.all_to_all(x, axes, split_axis=0, concat_axis=0, tiled=True)

    core = lax.axis_index("core").astype(jnp.int32).reshape(1)
    send, zn = call(
        first_kernel,
        [wide, ((POS, C), BF16)],
        [bf16(TILE, TILE, C), bf16(C, 5 * C), f32(4, C), pltpu.SemaphoreType.DMA((3,))],
        pair,
        w_in,
        norm_params,
        anywhere=True,
    )
    own = turn(send)
    sib = lax.ppermute(own, "core", swap)
    part, a_own, b_own = call(
        second_kernel,
        [((384, 256), F32), ((384, 256), BF16), ((COLS, 2, WIDE, 256), BF16)],
        [f32(tiles, 128), f32(1024, 128)],
        core,
        own,
        scalars=1,
    )
    (send,) = call(
        second_kernel_sib,
        [thin],
        [f32(tiles, 128), f32(1024, 128), bf16(384, 256), bf16(COLS, 2, WIDE, 256)],
        core,
        sib,
        part,
        scalars=1,
    )
    send, update, dp4, gwo, mid = call(
        third_kernel,
        [thin, ((TILE, TILE, C), BF16), ((C, POS), BF16), ((C, C), F32), ((8, 128), F32)],
        [],
        turn(send),
        zn,
        cotangent,
        w_in,
        w_out,
        norm_params,
    )
    own = turn(send)
    sib = lax.ppermute(own, "core", swap)
    scratch = [f32(tiles // 2, 128), bf16(384, 256), f32(512, 128)]
    da, db = call(
        fourth_kernel,
        [((384, 256), F32), ((tiles // 2, 128), F32)],
        scratch,
        core,
        own,
        a_own,
        b_own,
        scalars=1,
    )
    (send,) = call(
        fourth_kernel_sib, [wide], scratch + [f32(tiles // 2, 128)], core, sib, a_own, b_own, da, db, scalars=1
    )
    grad_pair, grads = call(
        fifth_kernel,
        [((TILE, TILE, C), BF16), chunks],
        [],
        turn(send),
        zn,
        pair,
        w_in,
        dp4,
        gwo,
        mid,
        norm_params,
    )
    (send,) = call(functools.partial(spread_kernel, scale=1.0), [((8, 32, C), BF16)], [], turn(grads, PLANE_AXES))
    (send,) = call(functools.partial(spread_kernel, scale=1.0 / 384.0), [chunks], [], turn(send, "z"))
    grad_w_in, grad_w_out, grad_norm = call(
        last_kernel, [((C, 5 * C), F32), ((C, C), F32), ((4, C), F32)], [], turn(send, PLANE_AXES)
    )
    return (update, grad_pair, grad_w_in, grad_w_out, grad_norm)


def solution(mesh):
    fine = Mesh(mesh.devices.reshape(8, 2, 4, 2, 2), CHIP_AXES + ("core",))
    tile = P(("z", "yl"), ("x", "yh", "core"), None)
    placed = (tile, tile, P(), P(), P())
    return jax.shard_map(shards, mesh=fine, in_specs=placed, out_specs=placed, check_vma=False)
```

```python
import functools

import jax
import jax.numpy as jnp
from jax import lax
from jax.experimental import pallas as pl
from jax.experimental.pallas import tpu as pltpu
from jax.sharding import Mesh
from jax.sharding import PartitionSpec as P

F32 = jnp.float32
BF16 = jnp.bfloat16
EPS = 1e-05
ROWS = 16
COLS = 8
CHIPS = 128
TILE = 24
WIDE = 32
TROWS = 5
POS = 128 * TROWS
C = 128
PLANE = 32
CHIP_AXES = ("x", "yh", "z", "yl")
PLANE_AXES = ("yl", "x", "yh", "core")


def dot(x, y, cx, cy):
    return lax.dot_general(x, y, (((cx,), (cy,)), ((), ())), preferred_element_type=F32)


def windows(rows):
    lane = lax.broadcasted_iota(jnp.int32, (rows, 128), 1)
    return lane, [((lane - 8 * n) & 127) < TILE for n in range(16)]


def block_turn(parts, wins, step, count, out_step, used):
    lane, masks = wins
    rolled = [p if a == 0 else pltpu.roll(p, step * a % 128, 1) for a, p in enumerate(parts)]
    outs = []
    for b in range(count):
        mixed = rolled[0]
        for a in range(1, len(parts)):
            mixed = jnp.where(masks[(step * a + out_step * b) % 128 // 8], rolled[a], mixed)
        if b:
            mixed = pltpu.roll(mixed, (128 - out_step * b) % 128, 1)
        outs.append(jnp.where(used, mixed, 0.0))
    return outs


def spread_turn(parts, wins, t):
    return block_turn(parts, wins, WIDE, min(5, TILE - 5 * t), TILE, (wins[0] & 31) < TILE)


def dense_turn(parts, wins):
    return block_turn(parts, wins, TILE, 4, WIDE, wins[0] < TILE * len(parts))


def rows_of(t):
    return range(5 * t, min(5 * t + 5, TILE))


def norm_lanes(v):
    mu = jnp.mean(v, axis=-1, keepdims=True)
    d = v - mu
    rstd = 1.0 / jnp.sqrt(jnp.mean(d * d, axis=-1, keepdims=True) + EPS)
    return d * rstd, rstd


def padded(tile):
    tile = tile.astype(F32)
    parts = []
    for t in range(TROWS):
        rows = len(rows_of(t))
        parts += [tile[5 * t : 5 * t + rows].reshape(rows * TILE, C), jnp.zeros((128 - rows * TILE, C), F32)]
    return jnp.concatenate(parts, axis=0)


def compact(val):
    parts = [val[128 * t : 128 * t + TILE * len(rows_of(t))].reshape(-1, TILE, C) for t in range(TROWS)]
    return jnp.concatenate(parts, axis=0)


def first_kernel(pair_hbm, w_hbm, norm_hbm, send_hbm, zn_hbm, pair_ref, w_ref, norm_ref, send_ref, zn_ref, sems):
    ends = ((pair_hbm, pair_ref), (norm_hbm, norm_ref), (w_hbm, w_ref), (zn_ref, zn_hbm))
    ends += tuple((send_ref.at[pl.ds(64 * n, 64)], send_hbm.at[pl.ds(64 * n, 64)]) for n in range(2))
    copies = [pltpu.make_async_copy(src, dst, sems.at[i]) for i, (src, dst) in enumerate(ends)]
    for copy in copies[:3]:
        copy.start()
    copies[0].wait()
    hat, _ = norm_lanes(pair_ref[...].astype(F32))
    copies[1].wait()
    zn = padded(hat * norm_ref[0:1, :][None] + norm_ref[1:2, :][None]).astype(BF16)
    zn_ref[...] = zn
    copies[3].start()
    copies[2].wait()
    p = [dot(w_ref[:, n * C : (n + 1) * C], zn, 0, 1) for n in range(4)]
    for n in range(2):
        part = slice(64 * n, 64 * n + 64)
        for m in range(2):
            send_ref[part, m, :] = (jax.nn.sigmoid(p[2 * m + 1][part]) * p[2 * m][part]).astype(BF16)
        copies[4 + n].start()
    for copy in copies[3:]:
        copy.wait()


def block(src, q, row, t):
    return src[pl.ds(ROWS * q, ROWS), row, t * 128 : (t + 1) * 128].astype(F32)


def tile_of(row, per, t):
    return (row, t) if per == TROWS else (t // per, t % per)


def gather_rows(src, row, per, dst):
    wins = windows(ROWS)
    for g in range(2):
        for t in range(TROWS):
            parts = [block(src, 4 * g + u, *tile_of(row, per, t)) for u in range(4)]
            for i, o in zip(rows_of(t), spread_turn(parts, wins, t)):
                dst[pl.ds(16 * i, 16), g * 128 : (g + 1) * 128] = o.astype(BF16)


def scatter_rows(val, dst, row, per):
    wins = windows(ROWS)
    for g in range(2):
        for t in range(TROWS):
            parts = [val[16 * i : 16 * i + 16, g * 128 : (g + 1) * 128] for i in rows_of(t)]
            s, lanes = tile_of(row, per, t)
            for u, o in enumerate(dense_turn(parts, wins)):
                dst[pl.ds(ROWS * (4 * g + u), ROWS), s, lanes * 128 : (lanes + 1) * 128] = o.astype(BF16)


def product(core, src, a_dst, b_dst, bscr):
    gather_rows(src, 0, TROWS, a_dst)
    for half in range(2 * 16):
        bscr[pl.ds(half * WIDE + TILE, WIDE - TILE), :] = jnp.zeros((WIDE - TILE, 128), F32)
    wins = windows(ROWS)
    for g in range(2):
        for t in range(TROWS):
            parts = [block(src, 4 * g + u, 1, t) for u in range(4)]
            for j, o in zip(rows_of(t), spread_turn(parts, wins, t)):
                bscr[pl.ds(512 * g + j, ROWS, stride=WIDE), :] = o
    for g in range(2):
        b_dst[:, :, :, g * 128 : (g + 1) * 128] = bscr[512 * g : 512 * g + 512, :].astype(BF16).reshape(COLS, 2, WIDE, 128)
    return dot(a_dst[...], b_dst[:, core].reshape(COLS * WIDE, 256), 1, 1)


def second_kernel(core_ref, src_ref, part_ref, a_ref, b_ref, bscr):
    part_ref[...] = product(core_ref[0], src_ref, a_ref, b_ref, bscr)


def second_kernel_sib(core_ref, src_ref, part_ref, send_ref, bscr, a_ref, b_ref):
    total = part_ref[...] + product(core_ref[0], src_ref, a_ref, b_ref, bscr)
    scatter_rows(total, send_ref, 0, 3)
    send_ref[:, 1, 256:] = jnp.zeros((CHIPS, 128), BF16)


def column(row):
    return jnp.broadcast_to(row, (C, C)).T[:, :1]


def lane_sums(val):
    part = val[:, :128]
    for t in range(1, TROWS):
        part = part + val[:, t * 128 : (t + 1) * 128]
    return jnp.sum(part.T, axis=0, keepdims=True)


def third_kernel(recv_ref, zn_ref, cot_ref, w_ref, wo_ref, norm_ref, send_ref, upd_ref, dp4_ref, gwo_ref, mid_ref):
    x = jnp.concatenate([recv_ref[:, s, :].astype(F32) for s in range(2)], axis=1)[:, :POS]
    gain, bias = column(norm_ref[2:3, :]), column(norm_ref[3:4, :])
    mu = jnp.mean(x, axis=0, keepdims=True)
    d = x - mu
    rstd = 1.0 / jnp.sqrt(jnp.mean(d * d, axis=0, keepdims=True) + EPS)
    hat = d * rstd
    xn = (hat * gain + bias).astype(BF16)
    y = dot(wo_ref[...], xn, 0, 0)
    gate = jax.nn.sigmoid(dot(w_ref[:, 4 * C :], zn_ref[...], 0, 1))
    upd = compact((gate * y).T)
    upd_ref[...] = upd.astype(BF16)
    cot = padded(cot_ref[...]).T
    cg = cot * gate
    dy = cg.astype(BF16)
    dp4_ref[...] = (cg * y * (1.0 - gate)).astype(BF16)
    gwo_ref[...] = dot(xn, dy, 1, 1)
    dxn = dot(wo_ref[...], dy, 1, 0)
    mid_ref[0:1, :] = lane_sums(dxn * hat)
    mid_ref[1:2, :] = lane_sums(dxn)
    mid_ref[2:8, :] = jnp.zeros((6, 128), F32)
    e = dxn * gain
    dx = rstd * (e - jnp.mean(e, axis=0, keepdims=True) - hat * jnp.mean(e * hat, axis=0, keepdims=True))
    dx = jnp.concatenate([dx, jnp.zeros((C, 768 - POS), F32)], axis=1)
    for half in range(2):
        send_ref[:, half, :] = dx[:, half * 384 : (half + 1) * 384].astype(BF16)


def back_product(side, src, a_ref, b_ref, d_ref, dbscr, sscr):
    gather_rows(src, 0, 3, d_ref)
    dx = d_ref[...]
    db = dot(dx, a_ref[...], 0, 0)
    for g in range(2):
        dbscr[pl.ds(256 * g, 256), :] = db[:, g * 128 : (g + 1) * 128]
    wins = windows(COLS)
    for g in range(2):
        for t in range(TROWS):
            parts = [dbscr[pl.ds(256 * g + j, COLS, stride=WIDE), :] for j in rows_of(t)]
            for u, o in enumerate(dense_turn(parts, wins)):
                sscr[pl.ds(t * CHIPS + ROWS * (4 * g + u) + side, COLS, stride=2), :] = o
    return dot(dx, b_ref[:, side].reshape(COLS * WIDE, 256), 1, 0)


def fourth_kernel(core_ref, src_ref, a_ref, b_ref, da_ref, db_ref, d_ref, dbscr):
    da_ref[...] = back_product(core_ref[0], src_ref, a_ref, b_ref, d_ref, dbscr, db_ref)


def fourth_kernel_sib(core_ref, src_ref, a_ref, b_ref, da_ref, db_ref, send_ref, d_ref, dbscr, sscr):
    core = core_ref[0]
    da = da_ref[...] + back_product(1 - core, src_ref, a_ref, b_ref, d_ref, dbscr, sscr)
    mine = lax.broadcasted_iota(jnp.int32, (CHIPS, 128), 0) % 2 == core
    for t in range(TROWS):
        tile = pl.ds(t * CHIPS, CHIPS)
        send_ref[:, 1, t * 128 : (t + 1) * 128] = jnp.where(mine, db_ref[tile, :], sscr[tile, :]).astype(BF16)
    scatter_rows(da, send_ref, 0, TROWS)


def fifth_kernel(recv_ref, zn_ref, pair_ref, w_ref, dp4_ref, gwo_ref, mid_ref, norm_ref, gpair_ref, g_ref):
    zn = zn_ref[...]
    blocks = []
    for m in range(2):
        grad = recv_ref[:, m, :].astype(F32)
        p = dot(w_ref[:, 2 * m * C : (2 * m + 2) * C], zn, 0, 1)
        s = jax.nn.sigmoid(p[C:])
        gs = grad * s
        blocks += [gs.astype(BF16), (gs * p[:C] * (1.0 - s)).astype(BF16)]
    dp = jnp.concatenate(blocks + [dp4_ref[...]], axis=0)
    dzn = dot(w_ref[...], dp, 1, 0).T
    hat, rstd = norm_lanes(padded(pair_ref[...]))
    e = dzn * norm_ref[0:1, :]
    back = rstd * (e - jnp.mean(e, axis=-1, keepdims=True) - hat * jnp.mean(e * hat, axis=-1, keepdims=True))
    gpair_ref[...] = compact(back).astype(BF16)
    first = jnp.sum(dzn * hat, axis=0, keepdims=True)
    second = jnp.sum(dzn, axis=0, keepdims=True)
    grads = jnp.concatenate([dot(dp, zn, 1, 0), gwo_ref[...]], axis=0).reshape(PLANE, 24, C)
    sums = jnp.concatenate([first, second, mid_ref[0:2, :], jnp.zeros((4, C), F32)], axis=0)[None]
    sums = jnp.concatenate([sums, jnp.zeros((PLANE - 1, 8, C), F32)], axis=0)
    g_ref[...] = jnp.concatenate([grads, sums], axis=1).astype(BF16)


def spread_kernel(recv_ref, send_ref, *, scale):
    total = jnp.sum(recv_ref[...].astype(F32), axis=0) * scale
    send_ref[...] = jnp.broadcast_to(total[None], send_ref.shape).astype(BF16)


def last_kernel(full_ref, gwi_ref, gwo_ref, gn_ref):
    full = full_ref[...].astype(F32)
    grads = full[:, :24, :].reshape(6 * C, C)
    for m in range(5):
        gwi_ref[:, m * C : (m + 1) * C] = grads[m * C : (m + 1) * C, :].T
    gwo_ref[...] = grads[5 * C :, :]
    gn_ref[...] = full[0, 24:28, :]


def call(kernel, outs, scratch, *args, scalars=0, anywhere=False):
    vmem = pl.BlockSpec(memory_space=pltpu.VMEM)
    smem = pl.BlockSpec(memory_space=pltpu.SMEM)
    rest = pl.BlockSpec(memory_space=pltpu.HBM) if anywhere else vmem
    return pl.pallas_call(
        kernel,
        out_shape=[jax.ShapeDtypeStruct(s, t) for s, t in outs],
        in_specs=[smem] * scalars + [rest] * (len(args) - scalars),
        out_specs=[rest] * len(outs),
        scratch_shapes=scratch,
        compiler_params=pltpu.CompilerParams(vmem_limit_bytes=62000000 if anywhere else 40 * 1024 * 1024),
    )(*args)


def shards(pair, cotangent, w_in, w_out, norm_params):
    swap = [(0, 1), (1, 0)]
    f32, bf16 = (lambda *s: pltpu.VMEM(s, F32)), (lambda *s: pltpu.VMEM(s, BF16))
    wide, thin = ((CHIPS, 2, POS), BF16), ((CHIPS, 2, 384), BF16)
    tiles = TROWS * CHIPS

    chunks = ((PLANE, 32, C), BF16)

    def turn(x, axes=CHIP_AXES):
        return lax.all_to_all(x, axes, split_axis=0, concat_axis=0, tiled=True)

    core = lax.axis_index("core").astype(jnp.int32).reshape(1)
    send, zn = call(
        first_kernel,
        [wide, ((POS, C), BF16)],
        [
            bf16(TILE, TILE, C),
            bf16(C, 5 * C),
            f32(4, C),
            bf16(CHIPS, 2, POS),
            bf16(POS, C),
            pltpu.SemaphoreType.DMA((6,)),
        ],
        pair,
        w_in,
        norm_params,
        anywhere=True,
    )
    own = turn(send)
    sib = lax.ppermute(own, "core", swap)
    part, a_own, b_own = call(
        second_kernel,
        [((384, 256), F32), ((384, 256), BF16), ((COLS, 2, WIDE, 256), BF16)],
        [f32(1024, 128)],
        core,
        own,
        scalars=1,
    )
    (send,) = call(
        second_kernel_sib,
        [thin],
        [f32(1024, 128), bf16(384, 256), bf16(COLS, 2, WIDE, 256)],
        core,
        sib,
        part,
        scalars=1,
    )
    send, update, dp4, gwo, mid = call(
        third_kernel,
        [thin, ((TILE, TILE, C), BF16), ((C, POS), BF16), ((C, C), F32), ((8, 128), F32)],
        [],
        turn(send),
        zn,
        cotangent,
        w_in,
        w_out,
        norm_params,
    )
    own = turn(send)
    sib = lax.ppermute(own, "core", swap)
    scratch = [bf16(384, 256), f32(512, 128)]
    da, db = call(
        fourth_kernel,
        [((384, 256), F32), ((tiles, 128), F32)],
        scratch,
        core,
        own,
        a_own,
        b_own,
        scalars=1,
    )
    (send,) = call(
        fourth_kernel_sib, [wide], scratch + [f32(tiles, 128)], core, sib, a_own, b_own, da, db, scalars=1
    )
    grad_pair, grads = call(
        fifth_kernel,
        [((TILE, TILE, C), BF16), chunks],
        [],
        turn(send),
        zn,
        pair,
        w_in,
        dp4,
        gwo,
        mid,
        norm_params,
    )
    (send,) = call(functools.partial(spread_kernel, scale=1.0), [((8, 32, C), BF16)], [], turn(grads, PLANE_AXES))
    (send,) = call(functools.partial(spread_kernel, scale=1.0 / 384.0), [chunks], [], turn(send, "z"))
    grad_w_in, grad_w_out, grad_norm = call(
        last_kernel, [((C, 5 * C), F32), ((C, C), F32), ((4, C), F32)], [], turn(send, PLANE_AXES)
    )
    return (update, grad_pair, grad_w_in, grad_w_out, grad_norm)


def solution(mesh):
    fine = Mesh(mesh.devices.reshape(8, 2, 4, 2, 2), ("z", "yl", "x", "yh", "core"))
    tile = P(("z", "yl"), ("x", "yh", "core"), None)
    placed = (tile, tile, P(), P(), P())
    return jax.shard_map(shards, mesh=fine, in_specs=placed, out_specs=placed, check_vma=False)
```

```python
import functools

import jax
import jax.numpy as jnp
from jax import lax
from jax.experimental import pallas as pl
from jax.experimental.pallas import tpu as pltpu
from jax.sharding import Mesh
from jax.sharding import PartitionSpec as P

F32 = jnp.float32
BF16 = jnp.bfloat16
EPS = 1e-05
ROWS = 16
COLS = 8
CHIPS = 128
TILE = 24
WIDE = 32
TROWS = 5
POS = 128 * TROWS
C = 128
PLANE = 32
CHIP_AXES = ("x", "yh", "z", "yl")
PLANE_AXES = ("yl", "x", "yh", "core")


def dot(x, y, cx, cy):
    return lax.dot_general(x, y, (((cx,), (cy,)), ((), ())), preferred_element_type=F32)


def windows(rows):
    lane = lax.broadcasted_iota(jnp.int32, (rows, 128), 1)
    return lane, [((lane - 8 * n) & 127) < TILE for n in range(16)]


def block_turn(parts, wins, step, count, out_step, used):
    lane, masks = wins
    rolled = [p if a == 0 else pltpu.roll(p, step * a % 128, 1) for a, p in enumerate(parts)]
    outs = []
    for b in range(count):
        mixed = rolled[0]
        for a in range(1, len(parts)):
            mixed = jnp.where(masks[(step * a + out_step * b) % 128 // 8], rolled[a], mixed)
        if b:
            mixed = pltpu.roll(mixed, (128 - out_step * b) % 128, 1)
        outs.append(jnp.where(used, mixed, 0.0))
    return outs


def spread_turn(parts, wins, t):
    return block_turn(parts, wins, WIDE, min(5, TILE - 5 * t), TILE, (wins[0] & 31) < TILE)


def dense_turn(parts, wins):
    return block_turn(parts, wins, TILE, 4, WIDE, wins[0] < TILE * len(parts))


def rows_of(t):
    return range(5 * t, min(5 * t + 5, TILE))


def norm_lanes(v):
    mu = jnp.mean(v, axis=-1, keepdims=True)
    d = v - mu
    rstd = 1.0 / jnp.sqrt(jnp.mean(d * d, axis=-1, keepdims=True) + EPS)
    return d * rstd, rstd


def padded(tile):
    tile = tile.astype(F32)
    parts = []
    for t in range(TROWS):
        rows = len(rows_of(t))
        parts += [tile[5 * t : 5 * t + rows].reshape(rows * TILE, C), jnp.zeros((128 - rows * TILE, C), F32)]
    return jnp.concatenate(parts, axis=0)


def compact(val):
    parts = [val[128 * t : 128 * t + TILE * len(rows_of(t))].reshape(-1, TILE, C) for t in range(TROWS)]
    return jnp.concatenate(parts, axis=0)


def first_kernel(pair_hbm, w_hbm, norm_hbm, send_ref, zn_ref, pair_ref, w_ref, norm_ref, sems):
    ends = ((pair_hbm, pair_ref), (norm_hbm, norm_ref), (w_hbm, w_ref))
    copies = [pltpu.make_async_copy(src, dst, sems.at[i]) for i, (src, dst) in enumerate(ends)]
    for copy in copies:
        copy.start()
    copies[0].wait()
    hat, _ = norm_lanes(pair_ref[...].astype(F32))
    copies[1].wait()
    zn = padded(hat * norm_ref[0:1, :][None] + norm_ref[1:2, :][None]).astype(BF16)
    zn_ref[...] = zn
    copies[2].wait()
    for m in range(2):
        p = dot(w_ref[:, 2 * m * C : (2 * m + 2) * C], zn, 0, 1)
        send_ref[:, m, :] = (jax.nn.sigmoid(p[C:]) * p[:C]).astype(BF16)


def block(src, q, row, t):
    return src[pl.ds(ROWS * q, ROWS), row, t * 128 : (t + 1) * 128].astype(F32)


def tile_of(row, per, t):
    return (row, t) if per == TROWS else (t // per, t % per)


def gather_rows(src, row, per, dst):
    wins = windows(ROWS)
    for g in range(2):
        for t in range(TROWS):
            parts = [block(src, 4 * g + u, *tile_of(row, per, t)) for u in range(4)]
            for i, o in zip(rows_of(t), spread_turn(parts, wins, t)):
                dst[pl.ds(16 * i, 16), g * 128 : (g + 1) * 128] = o.astype(BF16)


def scatter_rows(val, dst, row, per):
    wins = windows(ROWS)
    for g in range(2):
        for t in range(TROWS):
            parts = [val[16 * i : 16 * i + 16, g * 128 : (g + 1) * 128] for i in rows_of(t)]
            s, lanes = tile_of(row, per, t)
            for u, o in enumerate(dense_turn(parts, wins)):
                dst[pl.ds(ROWS * (4 * g + u), ROWS), s, lanes * 128 : (lanes + 1) * 128] = o.astype(BF16)


def product(core, src, a_dst, b_dst, bscr):
    gather_rows(src, 0, TROWS, a_dst)
    for half in range(2 * 16):
        bscr[pl.ds(half * WIDE + TILE, WIDE - TILE), :] = jnp.zeros((WIDE - TILE, 128), F32)
    wins = windows(ROWS)
    for g in range(2):
        for t in range(TROWS):
            parts = [block(src, 4 * g + u, 1, t) for u in range(4)]
            for j, o in zip(rows_of(t), spread_turn(parts, wins, t)):
                bscr[pl.ds(512 * g + j, ROWS, stride=WIDE), :] = o
    for g in range(2):
        b_dst[:, :, :, g * 128 : (g + 1) * 128] = bscr[512 * g : 512 * g + 512, :].astype(BF16).reshape(COLS, 2, WIDE, 128)
    return dot(a_dst[...], b_dst[:, core].reshape(COLS * WIDE, 256), 1, 1)


def second_kernel(core_ref, src_ref, part_ref, a_ref, b_ref, bscr):
    part_ref[...] = product(core_ref[0], src_ref, a_ref, b_ref, bscr)


def second_kernel_sib(core_ref, src_ref, part_ref, send_ref, bscr, a_ref, b_ref):
    total = part_ref[...] + product(core_ref[0], src_ref, a_ref, b_ref, bscr)
    scatter_rows(total, send_ref, 0, 3)
    send_ref[:, 1, 256:] = jnp.zeros((CHIPS, 128), BF16)


def column(row):
    return jnp.broadcast_to(row, (C, C)).T[:, :1]


def lane_sums(val):
    part = val[:, :128]
    for t in range(1, TROWS):
        part = part + val[:, t * 128 : (t + 1) * 128]
    return jnp.sum(part.T, axis=0, keepdims=True)


def third_kernel(recv_ref, zn_ref, cot_ref, w_ref, wo_ref, norm_ref, send_ref, upd_ref, dp4_ref, gwo_ref, mid_ref):
    x = jnp.concatenate([recv_ref[:, s, :].astype(F32) for s in range(2)], axis=1)[:, :POS]
    gain, bias = column(norm_ref[2:3, :]), column(norm_ref[3:4, :])
    mu = jnp.mean(x, axis=0, keepdims=True)
    d = x - mu
    rstd = 1.0 / jnp.sqrt(jnp.mean(d * d, axis=0, keepdims=True) + EPS)
    hat = d * rstd
    xn = (hat * gain + bias).astype(BF16)
    y = dot(wo_ref[...], xn, 0, 0)
    gate = jax.nn.sigmoid(dot(w_ref[:, 4 * C :], zn_ref[...], 0, 1))
    upd = compact((gate * y).T)
    upd_ref[...] = upd.astype(BF16)
    cot = padded(cot_ref[...]).T
    cg = cot * gate
    dy = cg.astype(BF16)
    dp4_ref[...] = (cg * y * (1.0 - gate)).astype(BF16)
    gwo_ref[...] = dot(xn, dy, 1, 1)
    dxn = dot(wo_ref[...], dy, 1, 0)
    mid_ref[0:1, :] = lane_sums(dxn * hat)
    mid_ref[1:2, :] = lane_sums(dxn)
    mid_ref[2:8, :] = jnp.zeros((6, 128), F32)
    e = dxn * gain
    dx = rstd * (e - jnp.mean(e, axis=0, keepdims=True) - hat * jnp.mean(e * hat, axis=0, keepdims=True))
    dx = jnp.concatenate([dx, jnp.zeros((C, 768 - POS), F32)], axis=1)
    for half in range(2):
        send_ref[:, half, :] = dx[:, half * 384 : (half + 1) * 384].astype(BF16)


def back_product(side, src, a_ref, b_ref, d_ref, dbscr, sscr):
    gather_rows(src, 0, 3, d_ref)
    dx = d_ref[...]
    db = dot(dx, a_ref[...], 0, 0)
    for g in range(2):
        dbscr[pl.ds(256 * g, 256), :] = db[:, g * 128 : (g + 1) * 128]
    wins = windows(COLS)
    for g in range(2):
        for t in range(TROWS):
            parts = [dbscr[pl.ds(256 * g + j, COLS, stride=WIDE), :] for j in rows_of(t)]
            for u, o in enumerate(dense_turn(parts, wins)):
                sscr[pl.ds(t * CHIPS + ROWS * (4 * g + u) + side, COLS, stride=2), :] = o
    return dot(dx, b_ref[:, side].reshape(COLS * WIDE, 256), 1, 0)


def fourth_kernel(core_ref, src_ref, a_ref, b_ref, da_ref, db_ref, d_ref, dbscr):
    da_ref[...] = back_product(core_ref[0], src_ref, a_ref, b_ref, d_ref, dbscr, db_ref)


def fourth_kernel_sib(core_ref, src_ref, a_ref, b_ref, da_ref, db_ref, send_ref, d_ref, dbscr, sscr):
    core = core_ref[0]
    da = da_ref[...] + back_product(1 - core, src_ref, a_ref, b_ref, d_ref, dbscr, sscr)
    mine = lax.broadcasted_iota(jnp.int32, (CHIPS, 128), 0) % 2 == core
    for t in range(TROWS):
        tile = pl.ds(t * CHIPS, CHIPS)
        send_ref[:, 1, t * 128 : (t + 1) * 128] = jnp.where(mine, db_ref[tile, :], sscr[tile, :]).astype(BF16)
    scatter_rows(da, send_ref, 0, TROWS)


def fifth_kernel(core_ref, recv_ref, zn_ref, w_ref, dp4_ref, gwo_ref, keep_ref, give_ref, dp_ref, scr):
    core = core_ref[0]
    zn = zn_ref[...]
    for m in range(2):
        grad = recv_ref[:, m, :].astype(F32)
        p = dot(w_ref[:, 2 * m * C : (2 * m + 2) * C], zn, 0, 1)
        s = jax.nn.sigmoid(p[C:])
        gs = grad * s
        dp_ref[2 * m * C : (2 * m + 1) * C, :] = gs.astype(BF16)
        dp_ref[(2 * m + 1) * C : (2 * m + 2) * C, :] = (gs * p[:C] * (1.0 - s)).astype(BF16)
    dp_ref[4 * C :, :] = dp4_ref[...]
    grads = dot(dp_ref[...], zn, 1, 0)
    scr[0] = grads[: 3 * C]
    scr[1, : 2 * C, :] = grads[3 * C :]
    scr[1, 2 * C :, :] = gwo_ref[...]
    keep_ref[...] = scr[core]
    give_ref[...] = scr[1 - core]


def sixth_kernel(dp_ref, pair_ref, w_ref, mid_ref, norm_ref, gpair_ref, sums_ref):
    dzn = dot(w_ref[...], dp_ref[...], 1, 0).T
    hat, rstd = norm_lanes(padded(pair_ref[...]))
    e = dzn * norm_ref[0:1, :]
    back = rstd * (e - jnp.mean(e, axis=-1, keepdims=True) - hat * jnp.mean(e * hat, axis=-1, keepdims=True))
    gpair_ref[...] = compact(back).astype(BF16)
    first = jnp.sum(dzn * hat, axis=0, keepdims=True)
    second = jnp.sum(dzn, axis=0, keepdims=True)
    sums_ref[...] = jnp.concatenate([first, second, mid_ref[0:2, :], jnp.zeros((4, C), F32)], axis=0)


def join_kernel(keep_ref, sib_ref, sums_ref, send_ref):
    grads = (keep_ref[...] + sib_ref[...]).reshape(PLANE // 2, 24, C)
    sums = jnp.concatenate([sums_ref[...][None], jnp.zeros((PLANE // 2 - 1, 8, C), F32)], axis=0)
    send_ref[...] = jnp.concatenate([grads, sums], axis=1).astype(BF16)


def spread_kernel(recv_ref, send_ref, *, scale):
    total = jnp.sum(recv_ref[...].astype(F32), axis=0) * scale
    send_ref[...] = jnp.broadcast_to(total[None], send_ref.shape).astype(BF16)


def last_kernel(full_ref, gwi_ref, gwo_ref, gn_ref):
    full = full_ref[...].astype(F32).reshape(PLANE // 2, 2, 32, C)
    halves = [full[:, h, :24, :].reshape(3 * C, C) for h in range(2)]
    for m in range(5):
        gwi_ref[:, m * C : (m + 1) * C] = halves[m // 3][m % 3 * C : (m % 3 + 1) * C, :].T
    gwo_ref[...] = halves[1][2 * C :, :]
    gn_ref[...] = full[0, 0, 24:28, :] + full[0, 1, 24:28, :]


def call(kernel, outs, scratch, *args, scalars=0, far=False):
    vmem = pl.BlockSpec(memory_space=pltpu.VMEM)
    smem = pl.BlockSpec(memory_space=pltpu.SMEM)
    rest = pl.BlockSpec(memory_space=pltpu.HBM) if far else vmem
    return pl.pallas_call(
        kernel,
        out_shape=[jax.ShapeDtypeStruct(s, t) for s, t in outs],
        in_specs=[smem] * scalars + [rest] * (len(args) - scalars),
        out_specs=[vmem] * len(outs),
        scratch_shapes=scratch,
        compiler_params=pltpu.CompilerParams(vmem_limit_bytes=40 * 1024 * 1024),
    )(*args)


def shards(pair, cotangent, w_in, w_out, norm_params):
    swap = [(0, 1), (1, 0)]
    f32, bf16 = (lambda *s: pltpu.VMEM(s, F32)), (lambda *s: pltpu.VMEM(s, BF16))
    wide, thin = ((CHIPS, 2, POS), BF16), ((CHIPS, 2, 384), BF16)
    tiles = TROWS * CHIPS

    chunks = ((PLANE, 32, C), BF16)

    def turn(x, axes=CHIP_AXES):
        return lax.all_to_all(x, axes, split_axis=0, concat_axis=0, tiled=True)

    core = lax.axis_index("core").astype(jnp.int32).reshape(1)
    send, zn = call(
        first_kernel,
        [wide, ((POS, C), BF16)],
        [bf16(TILE, TILE, C), bf16(C, 5 * C), f32(4, C), pltpu.SemaphoreType.DMA((3,))],
        *[pltpu.with_memory_space_constraint(v, pltpu.HBM) for v in (pair, w_in, norm_params)],
        far=True,
    )
    own = turn(send)
    sib = lax.ppermute(own, "core", swap)
    part, a_own, b_own = call(
        second_kernel,
        [((384, 256), F32), ((384, 256), BF16), ((COLS, 2, WIDE, 256), BF16)],
        [f32(1024, 128)],
        core,
        own,
        scalars=1,
    )
    (send,) = call(
        second_kernel_sib,
        [thin],
        [f32(1024, 128), bf16(384, 256), bf16(COLS, 2, WIDE, 256)],
        core,
        sib,
        part,
        scalars=1,
    )
    send, update, dp4, gwo, mid = call(
        third_kernel,
        [thin, ((TILE, TILE, C), BF16), ((C, POS), BF16), ((C, C), F32), ((8, 128), F32)],
        [],
        turn(send),
        zn,
        cotangent,
        w_in,
        w_out,
        norm_params,
    )
    own = turn(send)
    sib = lax.ppermute(own, "core", swap)
    scratch = [bf16(384, 256), f32(512, 128)]
    da, db = call(
        fourth_kernel,
        [((384, 256), F32), ((tiles, 128), F32)],
        scratch,
        core,
        own,
        a_own,
        b_own,
        scalars=1,
    )
    (send,) = call(
        fourth_kernel_sib, [wide], scratch + [f32(tiles, 128)], core, sib, a_own, b_own, da, db, scalars=1
    )
    half = ((3 * C, C), F32)
    keep, give, dp = call(
        fifth_kernel,
        [half, half, ((5 * C, POS), BF16)],
        [f32(2, 3 * C, C)],
        core,
        turn(send),
        zn,
        w_in,
        dp4,
        gwo,
        scalars=1,
    )
    sib = lax.ppermute(give, "core", swap)
    grad_pair, sums = call(
        sixth_kernel, [((TILE, TILE, C), BF16), ((8, C), F32)], [], dp, pair, w_in, mid, norm_params
    )
    (send,) = call(join_kernel, [((PLANE // 2, 32, C), BF16)], [], keep, sib, sums)
    send = turn(send, PLANE_AXES[:3])
    (send,) = call(functools.partial(spread_kernel, scale=1.0), [((8, 32, C), BF16)], [], send)
    (send,) = call(functools.partial(spread_kernel, scale=1.0 / 384.0), [chunks], [], turn(send, "z"))
    grad_w_in, grad_w_out, grad_norm = call(
        last_kernel, [((C, 5 * C), F32), ((C, C), F32), ((4, C), F32)], [], turn(send, PLANE_AXES)
    )
    return (update, grad_pair, grad_w_in, grad_w_out, grad_norm)


def solution(mesh):
    fine = Mesh(mesh.devices.reshape(8, 2, 4, 2, 2), ("z", "yl", "x", "yh", "core"))
    tile = P(("z", "yl"), ("x", "yh", "core"), None)
    placed = (tile, tile, P(), P(), P())
    return jax.shard_map(shards, mesh=fine, in_specs=placed, out_specs=placed, check_vma=False)
```

```python
import functools

import jax
import jax.numpy as jnp
from jax import lax
from jax.experimental import pallas as pl
from jax.experimental.pallas import tpu as pltpu
from jax.sharding import Mesh
from jax.sharding import PartitionSpec as P

F32 = jnp.float32
BF16 = jnp.bfloat16
EPS = 1e-05
ROWS = 16
COLS = 8
CHIPS = 128
TILE = 24
WIDE = 32
TROWS = 5
POS = 128 * TROWS
C = 128
PLANE = 32
CHIP_AXES = ("x", "yh", "yl", "z")
PLANE_AXES = ("yl", "x", "yh", "core")
FLIPS = {"x": 2, "yh": 1, "z": 4}


def dot(x, y, cx, cy):
    return lax.dot_general(x, y, (((cx,), (cy,)), ((), ())), preferred_element_type=F32)


def windows(rows):
    lane = lax.broadcasted_iota(jnp.int32, (rows, 128), 1)
    return lane, [((lane - 8 * n) & 127) < TILE for n in range(16)]


def block_turn(parts, wins, step, count, out_step, used):
    lane, masks = wins
    rolled = [p if a == 0 else pltpu.roll(p, step * a % 128, 1) for a, p in enumerate(parts)]
    outs = []
    for b in range(count):
        mixed = rolled[0]
        for a in range(1, len(parts)):
            mixed = jnp.where(masks[(step * a + out_step * b) % 128 // 8], rolled[a], mixed)
        if b:
            mixed = pltpu.roll(mixed, (128 - out_step * b) % 128, 1)
        outs.append(jnp.where(used, mixed, 0.0))
    return outs


def spread_turn(parts, wins, t):
    return block_turn(parts, wins, WIDE, min(5, TILE - 5 * t), TILE, (wins[0] & 31) < TILE)


def dense_turn(parts, wins):
    return block_turn(parts, wins, TILE, 4, WIDE, wins[0] < TILE * len(parts))


def rows_of(t):
    return range(5 * t, min(5 * t + 5, TILE))


def norm_lanes(v):
    mu = jnp.mean(v, axis=-1, keepdims=True)
    d = v - mu
    rstd = 1.0 / jnp.sqrt(jnp.mean(d * d, axis=-1, keepdims=True) + EPS)
    return d * rstd, rstd


def padded(tile):
    tile = tile.astype(F32)
    parts = []
    for t in range(TROWS):
        rows = len(rows_of(t))
        parts += [tile[5 * t : 5 * t + rows].reshape(rows * TILE, C), jnp.zeros((128 - rows * TILE, C), F32)]
    return jnp.concatenate(parts, axis=0)


def compact(val):
    parts = [val[128 * t : 128 * t + TILE * len(rows_of(t))].reshape(-1, TILE, C) for t in range(TROWS)]
    return jnp.concatenate(parts, axis=0)


def first_kernel(pair_hbm, w_hbm, norm_hbm, send_ref, zn_ref, pair_ref, w_ref, norm_ref, sems):
    ends = ((pair_hbm, pair_ref), (norm_hbm, norm_ref), (w_hbm, w_ref))
    copies = [pltpu.make_async_copy(src, dst, sems.at[i]) for i, (src, dst) in enumerate(ends)]
    for copy in copies:
        copy.start()
    copies[0].wait()
    hat, _ = norm_lanes(pair_ref[...].astype(F32))
    copies[1].wait()
    zn = padded(hat * norm_ref[0:1, :][None] + norm_ref[1:2, :][None]).astype(BF16)
    zn_ref[...] = zn
    copies[2].wait()
    for m in range(2):
        p = dot(w_ref[:, 2 * m * C : (2 * m + 2) * C], zn, 0, 1)
        send_ref[:, m, :] = (jax.nn.sigmoid(p[C:]) * p[:C]).astype(BF16)


def block(src, q, row, t, first=0, rows=ROWS):
    return src[pl.ds(ROWS * q + first, rows), row, t * 128 : (t + 1) * 128].astype(F32)


def tile_of(row, per, t):
    return (row, t) if per == TROWS else (t // per, t % per)


def gather_rows(src, row, per, dst):
    wins = windows(ROWS)
    for g in range(2):
        for t in range(TROWS):
            parts = [block(src, 4 * g + u, *tile_of(row, per, t)) for u in range(4)]
            for i, o in zip(rows_of(t), spread_turn(parts, wins, t)):
                dst[pl.ds(16 * i, 16), g * 128 : (g + 1) * 128] = o.astype(BF16)


def scatter_rows(val, scr):
    wins = windows(ROWS)
    for g in range(2):
        for t in range(TROWS):
            parts = [val[16 * i : 16 * i + 16, g * 128 : (g + 1) * 128] for i in rows_of(t)]
            for u, o in enumerate(dense_turn(parts, wins)):
                scr[ROWS * (4 * g + u) : ROWS * (4 * g + u + 1), t * 128 : (t + 1) * 128] = o


def swap_blocks(val):
    pairs = val.reshape(-1, 2, WIDE, val.shape[1])
    return jnp.concatenate([pairs[:, 1:], pairs[:, :1]], axis=1).reshape(val.shape)


def gather_b(src, first, rows, bscr, b_dst):
    for n in range(2 * rows):
        bscr[pl.ds(n * WIDE + TILE, WIDE - TILE), :] = jnp.zeros((WIDE - TILE, 128), F32)
    wins = windows(rows)
    for g in range(2):
        for t in range(TROWS):
            parts = [block(src, 4 * g + u, 1, t, first, rows) for u in range(4)]
            for j, o in zip(rows_of(t), spread_turn(parts, wins, t)):
                bscr[pl.ds(rows * WIDE * g + j, rows, stride=WIDE), :] = o
        part = swap_blocks(bscr[rows * WIDE * g : rows * WIDE * (g + 1), :]).astype(BF16)
        b_dst[:, :, g * 128 : (g + 1) * 128] = part.reshape(rows // COLS, COLS * WIDE, 128)


def second_kernel(core_ref, src_ref, part_ref, a_ref, b_ref, bscr):
    gather_rows(src_ref, 0, TROWS, a_ref)
    gather_b(src_ref, 0, ROWS, bscr, b_ref)
    part_ref[...] = dot(a_ref[...], b_ref[core_ref[0]], 1, 1)


def second_kernel_sib(core_ref, src_ref, part_ref, send_ref, bscr, a_ref, b_ref, scr):
    gather_rows(src_ref, 0, TROWS, a_ref)
    gather_b(src_ref, COLS * core_ref[0], COLS, bscr, b_ref)
    scatter_rows(part_ref[...] + dot(a_ref[...], b_ref[0], 1, 1), scr)
    for t in range(TROWS):
        send_ref[:, t // 3, t % 3 * 128 : (t % 3 + 1) * 128] = scr[:, t * 128 : (t + 1) * 128].astype(BF16)
    send_ref[:, 1, 256:] = jnp.zeros((CHIPS, 128), BF16)


def column(row):
    return jnp.broadcast_to(row, (C, C)).T[:, :1]


def lane_sums(val):
    part = val[:, :128]
    for t in range(1, TROWS):
        part = part + val[:, t * 128 : (t + 1) * 128]
    return jnp.sum(part.T, axis=0, keepdims=True)


def third_kernel(recv_ref, zn_ref, cot_ref, w_ref, wo_ref, norm_ref, send_ref, upd_ref, dp4_ref, gwo_ref, mid_ref):
    x = jnp.concatenate([recv_ref[:, s, :].astype(F32) for s in range(2)], axis=1)[:, :POS]
    gain, bias = column(norm_ref[2:3, :]), column(norm_ref[3:4, :])
    mu = jnp.mean(x, axis=0, keepdims=True)
    d = x - mu
    rstd = 1.0 / jnp.sqrt(jnp.mean(d * d, axis=0, keepdims=True) + EPS)
    hat = d * rstd
    xn = (hat * gain + bias).astype(BF16)
    y = dot(wo_ref[...], xn, 0, 0)
    gate = jax.nn.sigmoid(dot(w_ref[:, 4 * C :], zn_ref[...], 0, 1))
    upd = compact((gate * y).T)
    upd_ref[...] = upd.astype(BF16)
    cot = padded(cot_ref[...]).T
    cg = cot * gate
    dy = cg.astype(BF16)
    dp4_ref[...] = (cg * y * (1.0 - gate)).astype(BF16)
    gwo_ref[...] = dot(xn, dy, 1, 1)
    dxn = dot(wo_ref[...], dy, 1, 0)
    mid_ref[0:1, :] = lane_sums(dxn * hat)
    mid_ref[1:2, :] = lane_sums(dxn)
    mid_ref[2:8, :] = jnp.zeros((6, 128), F32)
    e = dxn * gain
    dx = rstd * (e - jnp.mean(e, axis=0, keepdims=True) - hat * jnp.mean(e * hat, axis=0, keepdims=True))
    dx = jnp.concatenate([dx, jnp.zeros((C, 768 - POS), F32)], axis=1)
    for half in range(2):
        send_ref[:, half, :] = dx[:, half * 384 : (half + 1) * 384].astype(BF16)


def back_product(side, src, a_ref, b_ref, d_ref, dbscr, store):
    gather_rows(src, 0, 3, d_ref)
    dx = d_ref[...]
    db = dot(dx, a_ref[...], 0, 0)
    for g in range(2):
        dbscr[pl.ds(256 * g, 256), :] = swap_blocks(db[:, g * 128 : (g + 1) * 128])
    wins = windows(COLS)
    for g in range(2):
        for t in range(TROWS):
            parts = [dbscr[pl.ds(256 * g + j, COLS, stride=WIDE), :] for j in rows_of(t)]
            for u, o in enumerate(dense_turn(parts, wins)):
                store(4 * g + u, slice(t * 128, (t + 1) * 128), o)
    return dot(dx, b_ref[side], 1, 0)


def fourth_kernel(core_ref, src_ref, a_ref, b_ref, da_ref, db_ref, d_ref, dbscr):
    def store(q, lanes, val):
        db_ref[COLS * q : COLS * (q + 1), lanes] = val

    da_ref[...] = back_product(core_ref[0], src_ref, a_ref, b_ref, d_ref, dbscr, store)


def fourth_kernel_sib(core_ref, src_ref, a_ref, b_ref, da_ref, db_ref, send_ref, d_ref, dbscr, scr):
    core = core_ref[0]

    def store(q, lanes, val):
        scr[pl.ds(pl.multiple_of(ROWS * q + COLS * (1 - core), COLS), COLS), lanes] = val

    da = da_ref[...] + back_product(1 - core, src_ref, a_ref, b_ref, d_ref, dbscr, store)
    for q in range(COLS):
        scr[pl.ds(pl.multiple_of(ROWS * q + COLS * core, COLS), COLS), :] = db_ref[COLS * q : COLS * (q + 1), :]
    send_ref[:, 1, :] = scr[...].astype(BF16)
    scatter_rows(da, scr)
    send_ref[:, 0, :] = scr[...].astype(BF16)


def fifth_kernel(core_ref, recv_ref, zn_ref, w_ref, dp4_ref, gwo_ref, keep_ref, give_ref, dp_ref, scr):
    core = core_ref[0]
    zn = zn_ref[...]
    for m in range(2):
        grad = recv_ref[:, m, :].astype(F32)
        p = dot(w_ref[:, 2 * m * C : (2 * m + 2) * C], zn, 0, 1)
        s = jax.nn.sigmoid(p[C:])
        gs = grad * s
        dp_ref[2 * m * C : (2 * m + 1) * C, :] = gs.astype(BF16)
        dp_ref[(2 * m + 1) * C : (2 * m + 2) * C, :] = (gs * p[:C] * (1.0 - s)).astype(BF16)
    dp_ref[4 * C :, :] = dp4_ref[...]
    grads = dot(dp_ref[...], zn, 1, 0)
    scr[0] = grads[: 3 * C]
    scr[1, : 2 * C, :] = grads[3 * C :]
    scr[1, 2 * C :, :] = gwo_ref[...]
    keep_ref[...] = scr[core]
    give_ref[...] = scr[1 - core]


def sixth_kernel(dp_ref, pair_ref, w_ref, mid_ref, norm_ref, gpair_ref, sums_ref):
    dzn = dot(w_ref[...], dp_ref[...], 1, 0).T
    hat, rstd = norm_lanes(padded(pair_ref[...]))
    e = dzn * norm_ref[0:1, :]
    back = rstd * (e - jnp.mean(e, axis=-1, keepdims=True) - hat * jnp.mean(e * hat, axis=-1, keepdims=True))
    gpair_ref[...] = compact(back).astype(BF16)
    first = jnp.sum(dzn * hat, axis=0, keepdims=True)
    second = jnp.sum(dzn, axis=0, keepdims=True)
    sums_ref[...] = jnp.concatenate([first, second, mid_ref[0:2, :], jnp.zeros((4, C), F32)], axis=0)


def join_kernel(keep_ref, sib_ref, sums_ref, send_ref):
    grads = (keep_ref[...] + sib_ref[...]).reshape(PLANE // 2, 24, C)
    sums = jnp.concatenate([sums_ref[...][None], jnp.zeros((PLANE // 2 - 1, 8, C), F32)], axis=0)
    send_ref[...] = jnp.concatenate([grads, sums], axis=1).astype(BF16)


def spread_kernel(recv_ref, send_ref, *, scale):
    total = jnp.sum(recv_ref[...].astype(F32), axis=0) * scale
    send_ref[...] = jnp.broadcast_to(total[None], send_ref.shape).astype(BF16)


def last_kernel(full_ref, gwi_ref, gwo_ref, gn_ref):
    full = full_ref[...].astype(F32).reshape(PLANE // 2, 2, 32, C)
    halves = [full[:, h, :24, :].reshape(3 * C, C) for h in range(2)]
    for m in range(5):
        gwi_ref[:, m * C : (m + 1) * C] = halves[m // 3][m % 3 * C : (m % 3 + 1) * C, :].T
    gwo_ref[...] = halves[1][2 * C :, :]
    gn_ref[...] = full[0, 0, 24:28, :] + full[0, 1, 24:28, :]


def call(kernel, outs, scratch, *args, scalars=0, far=False):
    vmem = pl.BlockSpec(memory_space=pltpu.VMEM)
    smem = pl.BlockSpec(memory_space=pltpu.SMEM)
    rest = pl.BlockSpec(memory_space=pltpu.HBM) if far else vmem
    return pl.pallas_call(
        kernel,
        out_shape=[jax.ShapeDtypeStruct(s, t) for s, t in outs],
        in_specs=[smem] * scalars + [rest] * (len(args) - scalars),
        out_specs=[vmem] * len(outs),
        scratch_shapes=scratch,
        compiler_params=pltpu.CompilerParams(vmem_limit_bytes=40 * 1024 * 1024),
    )(*args)


def shards(pair, cotangent, w_in, w_out, norm_params):
    swap = [(0, 1), (1, 0)]
    f32, bf16 = (lambda *s: pltpu.VMEM(s, F32)), (lambda *s: pltpu.VMEM(s, BF16))
    wide, thin = ((CHIPS, 2, POS), BF16), ((CHIPS, 2, 384), BF16)

    chunks = ((PLANE, 32, C), BF16)

    def turn(x, axes=CHIP_AXES):
        flip = 0
        for axis in axes:
            flip = flip * lax.axis_size(axis) + FLIPS.get(axis, 0)
        groups = [[n ^ flip for n in range(x.shape[0])]]
        return lax.all_to_all(x, axes, split_axis=0, concat_axis=0, axis_index_groups=groups, tiled=True)

    core = lax.axis_index("core").astype(jnp.int32).reshape(1)
    send, zn = call(
        first_kernel,
        [wide, ((POS, C), BF16)],
        [bf16(TILE, TILE, C), bf16(C, 5 * C), f32(4, C), pltpu.SemaphoreType.DMA((3,))],
        *[pltpu.with_memory_space_constraint(v, pltpu.HBM) for v in (pair, w_in, norm_params)],
        far=True,
    )
    own = turn(send)
    sib = lax.ppermute(own, "core", swap)
    part, a_own, b_own = call(
        second_kernel,
        [((384, 256), F32), ((384, 256), BF16), ((2, COLS * WIDE, 256), BF16)],
        [f32(1024, 128)],
        core,
        own,
        scalars=1,
    )
    (send,) = call(
        second_kernel_sib,
        [thin],
        [f32(512, 128), bf16(384, 256), bf16(1, COLS * WIDE, 256), f32(CHIPS, POS)],
        core,
        sib,
        part,
        scalars=1,
    )
    send, update, dp4, gwo, mid = call(
        third_kernel,
        [thin, ((TILE, TILE, C), BF16), ((C, POS), BF16), ((C, C), F32), ((8, 128), F32)],
        [],
        turn(send),
        zn,
        cotangent,
        w_in,
        w_out,
        norm_params,
    )
    own = turn(send)
    sib = lax.ppermute(own, "core", swap)
    scratch = [bf16(384, 256), f32(512, 128)]
    da, db = call(
        fourth_kernel,
        [((384, 256), F32), ((CHIPS // 2, POS), F32)],
        scratch,
        core,
        own,
        a_own,
        b_own,
        scalars=1,
    )
    (send,) = call(
        fourth_kernel_sib, [wide], scratch + [f32(CHIPS, POS)], core, sib, a_own, b_own, da, db, scalars=1
    )
    half = ((3 * C, C), F32)
    keep, give, dp = call(
        fifth_kernel,
        [half, half, ((5 * C, POS), BF16)],
        [f32(2, 3 * C, C)],
        core,
        turn(send),
        zn,
        w_in,
        dp4,
        gwo,
        scalars=1,
    )
    sib = lax.ppermute(give, "core", swap)
    grad_pair, sums = call(
        sixth_kernel, [((TILE, TILE, C), BF16), ((8, C), F32)], [], dp, pair, w_in, mid, norm_params
    )
    (send,) = call(join_kernel, [((PLANE // 2, 32, C), BF16)], [], keep, sib, sums)
    send = turn(send, PLANE_AXES[:3])
    (send,) = call(functools.partial(spread_kernel, scale=1.0), [((8, 32, C), BF16)], [], send)
    (send,) = call(functools.partial(spread_kernel, scale=1.0 / 384.0), [chunks], [], turn(send, ("z",)))
    grad_w_in, grad_w_out, grad_norm = call(
        last_kernel,
        [((C, 5 * C), F32), ((C, C), F32), ((4, C), F32)],
        [],
        turn(send, PLANE_AXES),
    )
    return (update, grad_pair, grad_w_in, grad_w_out, grad_norm)


def solution(mesh):
    fine = Mesh(mesh.devices.reshape(8, 2, 4, 2, 2), ("z", "yl", "x", "yh", "core"))
    tile = P(("z", "yl"), ("x", "yh", "core"), None)
    placed = (tile, tile, P(), P(), P())
    return jax.shard_map(shards, mesh=fine, in_specs=placed, out_specs=placed, check_vma=False)
```

```python
import functools

import jax
import jax.numpy as jnp
from jax import lax
from jax.experimental import pallas as pl
from jax.experimental.pallas import tpu as pltpu
from jax.sharding import Mesh
from jax.sharding import PartitionSpec as P

F32 = jnp.float32
BF16 = jnp.bfloat16
EPS = 1e-05
ROWS = 16
COLS = 8
CHIPS = 128
TILE = 24
WIDE = 32
TROWS = 5
POS = 128 * TROWS
C = 128
PLANE = 32
CHIP_AXES = ("x", "yh", "yl", "z")
PLANE_AXES = ("yl", "x", "yh", "core")
FLIPS = {"x": 2, "yh": 1, "z": 4}


def dot(x, y, cx, cy):
    return lax.dot_general(x, y, (((cx,), (cy,)), ((), ())), preferred_element_type=F32)


def windows(rows):
    lane = lax.broadcasted_iota(jnp.int32, (rows, 128), 1)
    return lane, [((lane - 8 * n) & 127) < TILE for n in range(16)]


def block_turn(parts, wins, step, count, out_step, used):
    lane, masks = wins
    rolled = [p if a == 0 else pltpu.roll(p, step * a % 128, 1) for a, p in enumerate(parts)]
    outs = []
    for b in range(count):
        mixed = rolled[0]
        for a in range(1, len(parts)):
            mixed = jnp.where(masks[(step * a + out_step * b) % 128 // 8], rolled[a], mixed)
        if b:
            mixed = pltpu.roll(mixed, (128 - out_step * b) % 128, 1)
        outs.append(jnp.where(used, mixed, 0.0))
    return outs


def spread_turn(parts, wins, t):
    return block_turn(parts, wins, WIDE, min(5, TILE - 5 * t), TILE, (wins[0] & 31) < TILE)


def dense_turn(parts, wins):
    return block_turn(parts, wins, TILE, 4, WIDE, wins[0] < TILE * len(parts))


def rows_of(t):
    return range(5 * t, min(5 * t + 5, TILE))


def norm_lanes(v):
    mu = jnp.mean(v, axis=-1, keepdims=True)
    d = v - mu
    rstd = 1.0 / jnp.sqrt(jnp.mean(d * d, axis=-1, keepdims=True) + EPS)
    return d * rstd, rstd


def padded(tile):
    tile = tile.astype(F32)
    parts = []
    for t in range(TROWS):
        rows = len(rows_of(t))
        parts += [tile[5 * t : 5 * t + rows].reshape(rows * TILE, C), jnp.zeros((128 - rows * TILE, C), F32)]
    return jnp.concatenate(parts, axis=0)


def compact(val):
    parts = [val[128 * t : 128 * t + TILE * len(rows_of(t))].reshape(-1, TILE, C) for t in range(TROWS)]
    return jnp.concatenate(parts, axis=0)


def first_kernel(pair_hbm, w_hbm, norm_hbm, send_ref, zn_ref, pair_ref, w_ref, norm_ref, sems):
    ends = ((pair_hbm, pair_ref), (norm_hbm, norm_ref), (w_hbm, w_ref))
    copies = [pltpu.make_async_copy(src, dst, sems.at[i]) for i, (src, dst) in enumerate(ends)]
    for copy in copies:
        copy.start()
    copies[0].wait()
    hat, _ = norm_lanes(pair_ref[...].astype(F32))
    copies[1].wait()
    zn = padded(hat * norm_ref[0:1, :][None] + norm_ref[1:2, :][None]).astype(BF16)
    zn_ref[...] = zn
    copies[2].wait()
    for m in range(2):
        p = dot(w_ref[:, 2 * m * C : (2 * m + 2) * C], zn, 0, 1)
        send_ref[:, m, :] = (jax.nn.sigmoid(p[C:]) * p[:C]).astype(BF16)


def block(src, q, row, t, first=0, rows=ROWS):
    return src[pl.ds(ROWS * q + first, rows), row, t * 128 : (t + 1) * 128].astype(F32)


def tile_of(row, per, t):
    return (row, t) if per == TROWS else (t // per, t % per)


def gather_rows(src, row, per, dst):
    wins = windows(ROWS)
    for g in range(2):
        for t in range(TROWS):
            parts = [block(src, 4 * g + u, *tile_of(row, per, t)) for u in range(4)]
            for i, o in zip(rows_of(t), spread_turn(parts, wins, t)):
                dst[pl.ds(16 * i, 16), g * 128 : (g + 1) * 128] = o.astype(BF16)


def scatter_rows(val, scr):
    wins = windows(ROWS)
    for g in range(2):
        for t in range(TROWS):
            parts = [val[16 * i : 16 * i + 16, g * 128 : (g + 1) * 128] for i in rows_of(t)]
            for u, o in enumerate(dense_turn(parts, wins)):
                scr[ROWS * (4 * g + u) : ROWS * (4 * g + u + 1), t * 128 : (t + 1) * 128] = o


def swap_blocks(val):
    pairs = val.reshape(-1, 2, WIDE, val.shape[1])
    return jnp.concatenate([pairs[:, 1:], pairs[:, :1]], axis=1).reshape(val.shape)


def gather_b(src, first, rows, bscr, b_dst):
    for n in range(2 * rows):
        bscr[pl.ds(n * WIDE + TILE, WIDE - TILE), :] = jnp.zeros((WIDE - TILE, 128), F32)
    wins = windows(rows)
    for g in range(2):
        for t in range(TROWS):
            parts = [block(src, 4 * g + u, 1, t, first, rows) for u in range(4)]
            for j, o in zip(rows_of(t), spread_turn(parts, wins, t)):
                bscr[pl.ds(rows * WIDE * g + j, rows, stride=WIDE), :] = o
        part = swap_blocks(bscr[rows * WIDE * g : rows * WIDE * (g + 1), :]).astype(BF16)
        b_dst[:, :, g * 128 : (g + 1) * 128] = part.reshape(rows // COLS, COLS * WIDE, 128)


def second_kernel(core_ref, src_ref, part_ref, a_ref, b_ref, bscr):
    gather_rows(src_ref, 0, TROWS, a_ref)
    gather_b(src_ref, 0, ROWS, bscr, b_ref)
    part_ref[...] = dot(a_ref[...], b_ref[core_ref[0]], 1, 1)


def second_kernel_sib(core_ref, src_ref, part_ref, send_ref, bscr, a_ref, b_ref, scr):
    gather_rows(src_ref, 0, TROWS, a_ref)
    gather_b(src_ref, COLS * core_ref[0], COLS, bscr, b_ref)
    scatter_rows(part_ref[...] + dot(a_ref[...], b_ref[0], 1, 1), scr)
    for t in range(TROWS):
        send_ref[:, t // 3, t % 3 * 128 : (t % 3 + 1) * 128] = scr[:, t * 128 : (t + 1) * 128].astype(BF16)
    send_ref[:, 1, 256:] = jnp.zeros((CHIPS, 128), BF16)


def column(row):
    return jnp.broadcast_to(row, (C, C)).T[:, :1]


def lane_sums(val):
    part = val[:, :128]
    for t in range(1, TROWS):
        part = part + val[:, t * 128 : (t + 1) * 128]
    return jnp.sum(part.T, axis=0, keepdims=True)


def third_kernel(recv_ref, zn_ref, cot_ref, w_ref, wo_ref, norm_ref, send_ref, upd_ref, dp4_ref, gwo_ref, mid_ref):
    x = jnp.concatenate([recv_ref[:, s, :].astype(F32) for s in range(2)], axis=1)[:, :POS]
    gain, bias = column(norm_ref[2:3, :]), column(norm_ref[3:4, :])
    mu = jnp.mean(x, axis=0, keepdims=True)
    d = x - mu
    rstd = 1.0 / jnp.sqrt(jnp.mean(d * d, axis=0, keepdims=True) + EPS)
    hat = d * rstd
    xn = (hat * gain + bias).astype(BF16)
    y = dot(wo_ref[...], xn, 0, 0)
    gate = jax.nn.sigmoid(dot(w_ref[:, 4 * C :], zn_ref[...], 0, 1))
    upd = compact((gate * y).T)
    upd_ref[...] = upd.astype(BF16)
    cot = padded(cot_ref[...]).T
    cg = cot * gate
    dy = cg.astype(BF16)
    dp4_ref[...] = (cg * y * (1.0 - gate)).astype(BF16)
    gwo_ref[...] = dot(xn, dy, 1, 1)
    dxn = dot(wo_ref[...], dy, 1, 0)
    mid_ref[0:1, :] = lane_sums(dxn * hat)
    mid_ref[1:2, :] = lane_sums(dxn)
    mid_ref[2:8, :] = jnp.zeros((6, 128), F32)
    e = dxn * gain
    dx = rstd * (e - jnp.mean(e, axis=0, keepdims=True) - hat * jnp.mean(e * hat, axis=0, keepdims=True))
    dx = jnp.concatenate([dx, jnp.zeros((C, 768 - POS), F32)], axis=1)
    for half in range(2):
        send_ref[:, half, :] = dx[:, half * 384 : (half + 1) * 384].astype(BF16)


def back_product(side, src, a_ref, b_ref, d_ref, dbscr, store):
    gather_rows(src, 0, 3, d_ref)
    dx = d_ref[...]
    db = dot(dx, a_ref[...], 0, 0)
    for g in range(2):
        dbscr[pl.ds(256 * g, 256), :] = swap_blocks(db[:, g * 128 : (g + 1) * 128])
    wins = windows(COLS)
    for g in range(2):
        for t in range(TROWS):
            parts = [dbscr[pl.ds(256 * g + j, COLS, stride=WIDE), :] for j in rows_of(t)]
            for u, o in enumerate(dense_turn(parts, wins)):
                store(4 * g + u, slice(t * 128, (t + 1) * 128), o)
    return dot(dx, b_ref[side], 1, 0)


def fourth_kernel(core_ref, src_ref, a_ref, b_ref, da_ref, db_ref, d_ref, dbscr):
    def store(q, lanes, val):
        db_ref[COLS * q : COLS * (q + 1), lanes] = val

    da_ref[...] = back_product(core_ref[0], src_ref, a_ref, b_ref, d_ref, dbscr, store)


def fourth_kernel_sib(core_ref, src_ref, a_ref, b_ref, da_ref, db_ref, send_ref, d_ref, dbscr, scr):
    core = core_ref[0]

    def store(q, lanes, val):
        scr[pl.ds(pl.multiple_of(ROWS * q + COLS * (1 - core), COLS), COLS), lanes] = val

    da = da_ref[...] + back_product(1 - core, src_ref, a_ref, b_ref, d_ref, dbscr, store)
    for q in range(COLS):
        scr[pl.ds(pl.multiple_of(ROWS * q + COLS * core, COLS), COLS), :] = db_ref[COLS * q : COLS * (q + 1), :]
    send_ref[:, 1, :] = scr[...].astype(BF16)
    scatter_rows(da, scr)
    send_ref[:, 0, :] = scr[...].astype(BF16)


def fifth_kernel(core_ref, recv_ref, zn_ref, w_ref, dp4_ref, gwo_ref, keep_ref, give_ref, dp_ref, scr):
    core = core_ref[0]
    zn = zn_ref[...]
    for m in range(2):
        grad = recv_ref[:, m, :].astype(F32)
        p = dot(w_ref[:, 2 * m * C : (2 * m + 2) * C], zn, 0, 1)
        s = jax.nn.sigmoid(p[C:])
        gs = grad * s
        dp_ref[2 * m * C : (2 * m + 1) * C, :] = gs.astype(BF16)
        dp_ref[(2 * m + 1) * C : (2 * m + 2) * C, :] = (gs * p[:C] * (1.0 - s)).astype(BF16)
    dp_ref[4 * C :, :] = dp4_ref[...]
    grads = dot(dp_ref[...], zn, 1, 0)
    scr[0] = grads[: 3 * C]
    scr[1, : 2 * C, :] = grads[3 * C :]
    scr[1, 2 * C :, :] = gwo_ref[...]
    keep_ref[...] = scr[core]
    give_ref[...] = scr[1 - core]


def sixth_kernel(dp_ref, pair_ref, w_ref, mid_ref, norm_ref, gpair_ref, sums_ref):
    dzn = dot(w_ref[...], dp_ref[...], 1, 0).T
    hat, rstd = norm_lanes(padded(pair_ref[...]))
    e = dzn * norm_ref[0:1, :]
    back = rstd * (e - jnp.mean(e, axis=-1, keepdims=True) - hat * jnp.mean(e * hat, axis=-1, keepdims=True))
    gpair_ref[...] = compact(back).astype(BF16)
    first = jnp.sum(dzn * hat, axis=0, keepdims=True)
    second = jnp.sum(dzn, axis=0, keepdims=True)
    sums_ref[...] = jnp.concatenate([first, second, mid_ref[0:2, :], jnp.zeros((4, C), F32)], axis=0)


def join_kernel(keep_ref, sib_ref, sums_ref, send_ref):
    grads = (keep_ref[...] + sib_ref[...]).reshape(PLANE // 2, 24, C)
    sums = jnp.concatenate([sums_ref[...][None], jnp.zeros((PLANE // 2 - 1, 8, C), F32)], axis=0)
    send_ref[...] = jnp.concatenate([grads, sums], axis=1).astype(BF16)


def spread_kernel(recv_ref, send_ref, *, scale):
    total = jnp.sum(recv_ref[...].astype(F32), axis=0) * scale
    send_ref[...] = jnp.broadcast_to(total[None], send_ref.shape).astype(BF16)


def last_kernel(full_ref, upd_ref, gpair_ref, gwi_ref, gwo_ref, gn_ref, upd_out, gpair_out):
    upd_out[...] = upd_ref[...]
    gpair_out[...] = gpair_ref[...]
    full = full_ref[...].astype(F32).reshape(PLANE // 2, 2, 32, C)
    halves = [full[:, h, :24, :].reshape(3 * C, C) for h in range(2)]
    for m in range(5):
        gwi_ref[:, m * C : (m + 1) * C] = halves[m // 3][m % 3 * C : (m % 3 + 1) * C, :].T
    gwo_ref[...] = halves[1][2 * C :, :]
    gn_ref[...] = full[0, 0, 24:28, :] + full[0, 1, 24:28, :]


def call(kernel, outs, scratch, *args, scalars=0, far=False):
    vmem = pl.BlockSpec(memory_space=pltpu.VMEM)
    smem = pl.BlockSpec(memory_space=pltpu.SMEM)
    rest = pl.BlockSpec(memory_space=pltpu.HBM) if far else vmem
    return pl.pallas_call(
        kernel,
        out_shape=[jax.ShapeDtypeStruct(s, t) for s, t in outs],
        in_specs=[smem] * scalars + [rest] * (len(args) - scalars),
        out_specs=[vmem] * len(outs),
        scratch_shapes=scratch,
        compiler_params=pltpu.CompilerParams(vmem_limit_bytes=40 * 1024 * 1024),
    )(*args)


def shards(pair, cotangent, w_in, w_out, norm_params):
    swap = [(0, 1), (1, 0)]
    f32, bf16 = (lambda *s: pltpu.VMEM(s, F32)), (lambda *s: pltpu.VMEM(s, BF16))
    wide, thin = ((CHIPS, 2, POS), BF16), ((CHIPS, 2, 384), BF16)

    chunks = ((PLANE, 32, C), BF16)

    def turn(x, axes=CHIP_AXES):
        flip = 0
        for axis in axes:
            flip = flip * lax.axis_size(axis) + FLIPS.get(axis, 0)
        groups = [[n ^ flip for n in range(x.shape[0])]]
        return lax.all_to_all(x, axes, split_axis=0, concat_axis=0, axis_index_groups=groups, tiled=True)

    core = lax.axis_index("core").astype(jnp.int32).reshape(1)
    send, zn = call(
        first_kernel,
        [wide, ((POS, C), BF16)],
        [bf16(TILE, TILE, C), bf16(C, 5 * C), f32(4, C), pltpu.SemaphoreType.DMA((3,))],
        *[pltpu.with_memory_space_constraint(v, pltpu.HBM) for v in (pair, w_in, norm_params)],
        far=True,
    )
    own = turn(send)
    sib = lax.ppermute(own, "core", swap)
    part, a_own, b_own = call(
        second_kernel,
        [((384, 256), F32), ((384, 256), BF16), ((2, COLS * WIDE, 256), BF16)],
        [f32(1024, 128)],
        core,
        own,
        scalars=1,
    )
    (send,) = call(
        second_kernel_sib,
        [thin],
        [f32(512, 128), bf16(384, 256), bf16(1, COLS * WIDE, 256), f32(CHIPS, POS)],
        core,
        sib,
        part,
        scalars=1,
    )
    send, update, dp4, gwo, mid = call(
        third_kernel,
        [thin, ((TILE, TILE, C), BF16), ((C, POS), BF16), ((C, C), F32), ((8, 128), F32)],
        [],
        turn(send),
        zn,
        cotangent,
        w_in,
        w_out,
        norm_params,
    )
    own = turn(send)
    sib = lax.ppermute(own, "core", swap)
    scratch = [bf16(384, 256), f32(512, 128)]
    da, db = call(
        fourth_kernel,
        [((384, 256), F32), ((CHIPS // 2, POS), F32)],
        scratch,
        core,
        own,
        a_own,
        b_own,
        scalars=1,
    )
    (send,) = call(
        fourth_kernel_sib, [wide], scratch + [f32(CHIPS, POS)], core, sib, a_own, b_own, da, db, scalars=1
    )
    half = ((3 * C, C), F32)
    keep, give, dp = call(
        fifth_kernel,
        [half, half, ((5 * C, POS), BF16)],
        [f32(2, 3 * C, C)],
        core,
        turn(send),
        zn,
        w_in,
        dp4,
        gwo,
        scalars=1,
    )
    sib = lax.ppermute(give, "core", swap)
    grad_pair, sums = call(
        sixth_kernel, [((TILE, TILE, C), BF16), ((8, C), F32)], [], dp, pair, w_in, mid, norm_params
    )
    (send,) = call(join_kernel, [((PLANE // 2, 32, C), BF16)], [], keep, sib, sums)
    send = turn(send, PLANE_AXES[:3])
    (send,) = call(functools.partial(spread_kernel, scale=1.0), [((8, 32, C), BF16)], [], send)
    (send,) = call(functools.partial(spread_kernel, scale=1.0 / 384.0), [chunks], [], turn(send, ("z",)))
    tile = ((TILE, TILE, C), BF16)
    grad_w_in, grad_w_out, grad_norm, update, grad_pair = call(
        last_kernel,
        [((C, 5 * C), F32), ((C, C), F32), ((4, C), F32), tile, tile],
        [],
        turn(send, PLANE_AXES),
        update,
        grad_pair,
    )
    return (update, grad_pair, grad_w_in, grad_w_out, grad_norm)


def solution(mesh):
    fine = Mesh(mesh.devices.reshape(8, 2, 4, 2, 2), ("z", "yl", "x", "yh", "core"))
    tile = P(("z", "yl"), ("x", "yh", "core"), None)
    placed = (tile, tile, P(), P(), P())
    return jax.shard_map(shards, mesh=fine, in_specs=placed, out_specs=placed, check_vma=False)
```

```python
import functools

import jax
import jax.numpy as jnp
from jax import lax
from jax.experimental import pallas as pl
from jax.experimental.pallas import tpu as pltpu
from jax.sharding import Mesh
from jax.sharding import PartitionSpec as P

F32 = jnp.float32
BF16 = jnp.bfloat16
EPS = 1e-05
ROWS = 16
COLS = 8
CHIPS = 128
TILE = 24
WIDE = 32
TROWS = 5
POS = 128 * TROWS
C = 128
PLANE = 32
CHIP_AXES = ("x", "yh", "yl", "z")
PLANE_AXES = ("yl", "x", "yh", "core")
FLIPS = {"x": 2, "yh": 1, "z": 4}


def dot(x, y, cx, cy):
    return lax.dot_general(x, y, (((cx,), (cy,)), ((), ())), preferred_element_type=F32)


def windows(rows):
    lane = lax.broadcasted_iota(jnp.int32, (rows, 128), 1)
    return lane, [((lane - 8 * n) & 127) < TILE for n in range(16)]


def block_turn(parts, wins, step, count, out_step, used):
    lane, masks = wins
    rolled = [p if a == 0 else pltpu.roll(p, step * a % 128, 1) for a, p in enumerate(parts)]
    outs = []
    for b in range(count):
        mixed = rolled[0]
        for a in range(1, len(parts)):
            mixed = jnp.where(masks[(step * a + out_step * b) % 128 // 8], rolled[a], mixed)
        if b:
            mixed = pltpu.roll(mixed, (128 - out_step * b) % 128, 1)
        outs.append(jnp.where(used, mixed, 0.0))
    return outs


def spread_turn(parts, wins, t):
    return block_turn(parts, wins, WIDE, min(5, TILE - 5 * t), TILE, (wins[0] & 31) < TILE)


def dense_turn(parts, wins):
    return block_turn(parts, wins, TILE, 4, WIDE, wins[0] < TILE * len(parts))


def rows_of(t):
    return range(5 * t, min(5 * t + 5, TILE))


def norm_lanes(v):
    mu = jnp.mean(v, axis=-1, keepdims=True)
    d = v - mu
    rstd = 1.0 / jnp.sqrt(jnp.mean(d * d, axis=-1, keepdims=True) + EPS)
    return d * rstd, rstd


def padded(tile):
    tile = tile.astype(F32)
    parts = []
    for t in range(TROWS):
        rows = len(rows_of(t))
        parts += [tile[5 * t : 5 * t + rows].reshape(rows * TILE, C), jnp.zeros((128 - rows * TILE, C), F32)]
    return jnp.concatenate(parts, axis=0)


def compact(val):
    parts = [val[128 * t : 128 * t + TILE * len(rows_of(t))].reshape(-1, TILE, C) for t in range(TROWS)]
    return jnp.concatenate(parts, axis=0)


def first_kernel(pair_hbm, w_hbm, norm_hbm, send_ref, zn_ref, pair_ref, w_ref, norm_ref, sems):
    ends = ((pair_hbm, pair_ref), (norm_hbm, norm_ref), (w_hbm, w_ref))
    copies = [pltpu.make_async_copy(src, dst, sems.at[i]) for i, (src, dst) in enumerate(ends)]
    for copy in copies:
        copy.start()
    copies[0].wait()
    hat, _ = norm_lanes(pair_ref[...].astype(F32))
    copies[1].wait()
    zn = padded(hat * norm_ref[0:1, :][None] + norm_ref[1:2, :][None]).astype(BF16)
    zn_ref[...] = zn
    copies[2].wait()
    for m in range(2):
        p = dot(w_ref[:, 2 * m * C : (2 * m + 2) * C], zn, 0, 1)
        send_ref[:, m, :] = (jax.nn.sigmoid(p[C:]) * p[:C]).astype(BF16)


def block(src, q, row, t, first=0, rows=ROWS):
    return src[pl.ds(ROWS * q + first, rows), row, t * 128 : (t + 1) * 128].astype(F32)


def tile_of(row, per, t):
    return (row, t) if per == TROWS else (t // per, t % per)


def gather_rows(src, row, per, dst):
    wins = windows(ROWS)
    for g in range(2):
        for t in range(TROWS):
            parts = [block(src, 4 * g + u, *tile_of(row, per, t)) for u in range(4)]
            for i, o in zip(rows_of(t), spread_turn(parts, wins, t)):
                dst[pl.ds(16 * i, 16), g * 128 : (g + 1) * 128] = o.astype(BF16)


def scatter_rows(val, scr):
    wins = windows(ROWS)
    for g in range(2):
        for t in range(TROWS):
            parts = [val[16 * i : 16 * i + 16, g * 128 : (g + 1) * 128] for i in rows_of(t)]
            for u, o in enumerate(dense_turn(parts, wins)):
                scr[ROWS * (4 * g + u) : ROWS * (4 * g + u + 1), t * 128 : (t + 1) * 128] = o


def swap_blocks(val):
    pairs = val.reshape(-1, 2, WIDE, val.shape[1])
    return jnp.concatenate([pairs[:, 1:], pairs[:, :1]], axis=1).reshape(val.shape)


def gather_b(src, first, rows, bscr, b_dst):
    for n in range(2 * rows):
        bscr[pl.ds(n * WIDE + TILE, WIDE - TILE), :] = jnp.zeros((WIDE - TILE, 128), F32)
    wins = windows(rows)
    for g in range(2):
        for t in range(TROWS):
            parts = [block(src, 4 * g + u, 1, t, first, rows) for u in range(4)]
            for j, o in zip(rows_of(t), spread_turn(parts, wins, t)):
                bscr[pl.ds(rows * WIDE * g + j, rows, stride=WIDE), :] = o
        part = swap_blocks(bscr[rows * WIDE * g : rows * WIDE * (g + 1), :]).astype(BF16)
        b_dst[:, :, g * 128 : (g + 1) * 128] = part.reshape(rows // COLS, COLS * WIDE, 128)


def second_kernel(core_ref, src_ref, part_ref, a_ref, b_ref, bscr):
    gather_rows(src_ref, 0, TROWS, a_ref)
    gather_b(src_ref, 0, ROWS, bscr, b_ref)
    part_ref[...] = dot(a_ref[...], b_ref[core_ref[0]], 1, 1)


def second_kernel_sib(core_ref, src_ref, part_ref, send_ref, bscr, a_ref, b_ref, scr):
    gather_rows(src_ref, 0, TROWS, a_ref)
    gather_b(src_ref, COLS * core_ref[0], COLS, bscr, b_ref)
    scatter_rows(part_ref[...] + dot(a_ref[...], b_ref[0], 1, 1), scr)
    for t in range(TROWS):
        send_ref[:, t // 3, t % 3 * 128 : (t % 3 + 1) * 128] = scr[:, t * 128 : (t + 1) * 128].astype(BF16)
    send_ref[:, 1, 256:] = jnp.zeros((CHIPS, 128), BF16)


def column(row):
    return jnp.broadcast_to(row, (C, C)).T[:, :1]


def lane_sums(val):
    part = val[:, :128]
    for t in range(1, TROWS):
        part = part + val[:, t * 128 : (t + 1) * 128]
    return jnp.sum(part.T, axis=0, keepdims=True)


def third_kernel(recv_ref, zn_ref, cot_ref, w_ref, wo_ref, norm_ref, send_ref, upd_ref, dp4_ref, gwo_ref, mid_ref):
    x = jnp.concatenate([recv_ref[:, s, :].astype(F32) for s in range(2)], axis=1)[:, :POS]
    gain, bias = column(norm_ref[2:3, :]), column(norm_ref[3:4, :])
    mu = jnp.mean(x, axis=0, keepdims=True)
    d = x - mu
    rstd = 1.0 / jnp.sqrt(jnp.mean(d * d, axis=0, keepdims=True) + EPS)
    hat = d * rstd
    xn = (hat * gain + bias).astype(BF16)
    y = dot(wo_ref[...], xn, 0, 0)
    gate = jax.nn.sigmoid(dot(w_ref[:, 4 * C :], zn_ref[...], 0, 1))
    upd = compact((gate * y).T)
    upd_ref[...] = upd.astype(BF16)
    cot = padded(cot_ref[...]).T
    cg = cot * gate
    dy = cg.astype(BF16)
    dp4_ref[...] = (cg * y * (1.0 - gate)).astype(BF16)
    gwo_ref[...] = dot(xn, dy, 1, 1)
    dxn = dot(wo_ref[...], dy, 1, 0)
    mid_ref[0:1, :] = lane_sums(dxn * hat)
    mid_ref[1:2, :] = lane_sums(dxn)
    mid_ref[2:8, :] = jnp.zeros((6, 128), F32)
    e = dxn * gain
    dx = rstd * (e - jnp.mean(e, axis=0, keepdims=True) - hat * jnp.mean(e * hat, axis=0, keepdims=True))
    dx = jnp.concatenate([dx, jnp.zeros((C, 768 - POS), F32)], axis=1)
    for half in range(2):
        send_ref[:, half, :] = dx[:, half * 384 : (half + 1) * 384].astype(BF16)


def back_product(side, src, a_ref, b_ref, d_ref, dbscr, store):
    gather_rows(src, 0, 3, d_ref)
    dx = d_ref[...]
    db = dot(dx, a_ref[...], 0, 0)
    for g in range(2):
        dbscr[pl.ds(256 * g, 256), :] = swap_blocks(db[:, g * 128 : (g + 1) * 128])
    wins = windows(COLS)
    for g in range(2):
        for t in range(TROWS):
            parts = [dbscr[pl.ds(256 * g + j, COLS, stride=WIDE), :] for j in rows_of(t)]
            for u, o in enumerate(dense_turn(parts, wins)):
                store(4 * g + u, slice(t * 128, (t + 1) * 128), o)
    return dot(dx, b_ref[side], 1, 0)


def fourth_kernel(core_ref, src_ref, a_ref, b_ref, da_ref, db_ref, d_ref, dbscr):
    def store(q, lanes, val):
        db_ref[COLS * q : COLS * (q + 1), lanes] = val

    da_ref[...] = back_product(core_ref[0], src_ref, a_ref, b_ref, d_ref, dbscr, store)


def fourth_kernel_sib(core_ref, src_ref, a_ref, b_ref, da_ref, db_ref, send_ref, d_ref, dbscr, scr):
    core = core_ref[0]

    def store(q, lanes, val):
        scr[pl.ds(pl.multiple_of(ROWS * q + COLS * (1 - core), COLS), COLS), lanes] = val

    da = da_ref[...] + back_product(1 - core, src_ref, a_ref, b_ref, d_ref, dbscr, store)
    for q in range(COLS):
        scr[pl.ds(pl.multiple_of(ROWS * q + COLS * core, COLS), COLS), :] = db_ref[COLS * q : COLS * (q + 1), :]
    send_ref[:, 1, :] = scr[...].astype(BF16)
    scatter_rows(da, scr)
    send_ref[:, 0, :] = scr[...].astype(BF16)


def fifth_kernel(core_ref, recv_ref, zn_ref, w_ref, dp4_ref, gwo_ref, keep_ref, give_ref, dp_ref, scr):
    core = core_ref[0]
    zn = zn_ref[...]
    for m in range(2):
        grad = recv_ref[:, m, :].astype(F32)
        p = dot(w_ref[:, 2 * m * C : (2 * m + 2) * C], zn, 0, 1)
        s = jax.nn.sigmoid(p[C:])
        gs = grad * s
        dp_ref[2 * m * C : (2 * m + 1) * C, :] = gs.astype(BF16)
        dp_ref[(2 * m + 1) * C : (2 * m + 2) * C, :] = (gs * p[:C] * (1.0 - s)).astype(BF16)
    dp_ref[4 * C :, :] = dp4_ref[...]
    grads = dot(dp_ref[...], zn, 1, 0)
    scr[0] = grads[: 3 * C]
    scr[1, : 2 * C, :] = grads[3 * C :]
    scr[1, 2 * C :, :] = gwo_ref[...]
    keep_ref[...] = scr[core]
    give_ref[...] = scr[1 - core]


def sixth_kernel(dp_ref, pair_ref, w_ref, mid_ref, norm_ref, gpair_ref, sums_ref):
    dzn = dot(w_ref[...], dp_ref[...], 1, 0).T
    hat, rstd = norm_lanes(padded(pair_ref[...]))
    e = dzn * norm_ref[0:1, :]
    back = rstd * (e - jnp.mean(e, axis=-1, keepdims=True) - hat * jnp.mean(e * hat, axis=-1, keepdims=True))
    gpair_ref[...] = compact(back).astype(BF16)
    first = jnp.sum(dzn * hat, axis=0, keepdims=True)
    second = jnp.sum(dzn, axis=0, keepdims=True)
    sums_ref[...] = jnp.concatenate([first, second, mid_ref[0:2, :], jnp.zeros((4, C), F32)], axis=0)


def join_kernel(keep_ref, sib_ref, sums_ref, send_ref):
    grads = (keep_ref[...] + sib_ref[...]).reshape(PLANE // 2, 24, C)
    sums = jnp.concatenate([sums_ref[...][None], jnp.zeros((PLANE // 2 - 1, 8, C), F32)], axis=0)
    send_ref[...] = jnp.concatenate([grads, sums], axis=1).astype(BF16)


def spread_kernel(recv_ref, send_ref, *, scale):
    total = jnp.sum(recv_ref[...].astype(F32), axis=0) * scale
    send_ref[...] = jnp.broadcast_to(total[None], send_ref.shape).astype(BF16)


def last_kernel(full_ref, upd_ref, gpair_ref, gwi_ref, gwo_ref, gn_ref, upd_out, gpair_out):
    upd_out[...] = upd_ref[...]
    gpair_out[...] = gpair_ref[...]
    full = full_ref[...].astype(F32).reshape(PLANE // 2, 2, 32, C)
    halves = [full[:, h, :24, :].reshape(3 * C, C) for h in range(2)]
    for m in range(5):
        gwi_ref[:, m * C : (m + 1) * C] = halves[m // 3][m % 3 * C : (m % 3 + 1) * C, :].T
    gwo_ref[...] = halves[1][2 * C :, :]
    gn_ref[...] = full[0, 0, 24:28, :] + full[0, 1, 24:28, :]


def call(kernel, outs, scratch, *args, scalars=0, far=False):
    vmem = pl.BlockSpec(memory_space=pltpu.VMEM)
    smem = pl.BlockSpec(memory_space=pltpu.SMEM)
    rest = pl.BlockSpec(memory_space=pltpu.HBM) if far else vmem
    return pl.pallas_call(
        kernel,
        out_shape=[jax.ShapeDtypeStruct(s, t) for s, t in outs],
        in_specs=[smem] * scalars + [rest] * (len(args) - scalars),
        out_specs=[vmem] * len(outs),
        scratch_shapes=scratch,
        compiler_params=pltpu.CompilerParams(vmem_limit_bytes=40 * 1024 * 1024),
    )(*args)


def shards(pair, cotangent, w_in, w_out, norm_params):
    swap = [(0, 1), (1, 0)]
    f32, bf16 = (lambda *s: pltpu.VMEM(s, F32)), (lambda *s: pltpu.VMEM(s, BF16))
    wide, thin = ((CHIPS, 2, POS), BF16), ((CHIPS, 2, 384), BF16)

    chunks = ((PLANE, 32, C), BF16)

    def turn(x, axes=CHIP_AXES):
        flip = 0
        for axis in axes:
            flip = flip * lax.axis_size(axis) + FLIPS.get(axis, 0)
        groups = [[n ^ flip for n in range(x.shape[0])]]
        return lax.all_to_all(x, axes, split_axis=0, concat_axis=0, axis_index_groups=groups, tiled=True)

    core = lax.axis_index("core").astype(jnp.int32).reshape(1)
    send, zn = call(
        first_kernel,
        [wide, ((POS, C), BF16)],
        [bf16(TILE, TILE, C), bf16(C, 5 * C), f32(4, C), pltpu.SemaphoreType.DMA((3,))],
        *[pltpu.with_memory_space_constraint(v, pltpu.HBM) for v in (pair, w_in, norm_params)],
        far=True,
    )
    own = turn(send)
    sib = lax.ppermute(own, "core", swap)
    part, a_own, b_own = call(
        second_kernel,
        [((384, 256), F32), ((384, 256), BF16), ((2, COLS * WIDE, 256), BF16)],
        [f32(1024 + WIDE, 128)],
        core,
        own,
        scalars=1,
    )
    (send,) = call(
        second_kernel_sib,
        [thin],
        [f32(512 + WIDE, 128), bf16(384, 256), bf16(1, COLS * WIDE, 256), f32(CHIPS, POS)],
        core,
        sib,
        part,
        scalars=1,
    )
    send, update, dp4, gwo, mid = call(
        third_kernel,
        [thin, ((TILE, TILE, C), BF16), ((C, POS), BF16), ((C, C), F32), ((8, 128), F32)],
        [],
        turn(send),
        zn,
        cotangent,
        w_in,
        w_out,
        norm_params,
    )
    own = turn(send)
    sib = lax.ppermute(own, "core", swap)
    scratch = [bf16(384, 256), f32(512 + WIDE, 128)]
    da, db = call(
        fourth_kernel,
        [((384, 256), F32), ((CHIPS // 2, POS), F32)],
        scratch,
        core,
        own,
        a_own,
        b_own,
        scalars=1,
    )
    (send,) = call(
        fourth_kernel_sib, [wide], scratch + [f32(CHIPS, POS)], core, sib, a_own, b_own, da, db, scalars=1
    )
    half = ((3 * C, C), F32)
    keep, give, dp = call(
        fifth_kernel,
        [half, half, ((5 * C, POS), BF16)],
        [f32(2, 3 * C, C)],
        core,
        turn(send),
        zn,
        w_in,
        dp4,
        gwo,
        scalars=1,
    )
    sib = lax.ppermute(give, "core", swap)
    grad_pair, sums = call(
        sixth_kernel, [((TILE, TILE, C), BF16), ((8, C), F32)], [], dp, pair, w_in, mid, norm_params
    )
    (send,) = call(join_kernel, [((PLANE // 2, 32, C), BF16)], [], keep, sib, sums)
    send = turn(send, PLANE_AXES[:3])
    (send,) = call(functools.partial(spread_kernel, scale=1.0), [((8, 32, C), BF16)], [], send)
    (send,) = call(functools.partial(spread_kernel, scale=1.0 / 384.0), [chunks], [], turn(send, ("z",)))
    tile = ((TILE, TILE, C), BF16)
    grad_w_in, grad_w_out, grad_norm, update, grad_pair = call(
        last_kernel,
        [((C, 5 * C), F32), ((C, C), F32), ((4, C), F32), tile, tile],
        [],
        turn(send, PLANE_AXES),
        update,
        grad_pair,
    )
    return (update, grad_pair, grad_w_in, grad_w_out, grad_norm)


def solution(mesh):
    fine = Mesh(mesh.devices.reshape(8, 2, 4, 2, 2), ("z", "yl", "x", "yh", "core"))
    tile = P(("z", "yl"), ("x", "yh", "core"), None)
    placed = (tile, tile, P(), P(), P())
    return jax.shard_map(shards, mesh=fine, in_specs=placed, out_specs=placed, check_vma=False)
```

```python
import functools

import jax
import jax.numpy as jnp
from jax import lax
from jax.experimental import pallas as pl
from jax.experimental.pallas import tpu as pltpu
from jax.sharding import Mesh
from jax.sharding import PartitionSpec as P

F32 = jnp.float32
BF16 = jnp.bfloat16
EPS = 1e-05
ROWS = 16
COLS = 8
CHIPS = 128
TILE = 24
WIDE = 32
TROWS = 5
POS = 128 * TROWS
C = 128
PLANE = 32
CHIP_AXES = ("x", "yh", "yl", "z")
PLANE_AXES = ("yl", "x", "yh", "core")
FLIPS = {"x": 2, "yh": 1, "z": 4}


def dot(x, y, cx, cy):
    return lax.dot_general(x, y, (((cx,), (cy,)), ((), ())), preferred_element_type=F32)


def windows(rows):
    lane = lax.broadcasted_iota(jnp.int32, (rows, 128), 1)
    return lane, [((lane - 8 * n) & 127) < TILE for n in range(16)]


def block_turn(parts, wins, step, count, out_step, used):
    lane, masks = wins
    rolled = [p if a == 0 else pltpu.roll(p, step * a % 128, 1) for a, p in enumerate(parts)]
    outs = []
    for b in range(count):
        mixed = rolled[0]
        for a in range(1, len(parts)):
            mixed = jnp.where(masks[(step * a + out_step * b) % 128 // 8], rolled[a], mixed)
        if b:
            mixed = pltpu.roll(mixed, (128 - out_step * b) % 128, 1)
        outs.append(jnp.where(used, mixed, 0.0))
    return outs


def spread_turn(parts, wins, t):
    return block_turn(parts, wins, WIDE, min(5, TILE - 5 * t), TILE, (wins[0] & 31) < TILE)


def dense_turn(parts, wins):
    return block_turn(parts, wins, TILE, 4, WIDE, wins[0] < TILE * len(parts))


def rows_of(t):
    return range(5 * t, min(5 * t + 5, TILE))


def norm_lanes(v):
    mu = jnp.mean(v, axis=-1, keepdims=True)
    d = v - mu
    rstd = 1.0 / jnp.sqrt(jnp.mean(d * d, axis=-1, keepdims=True) + EPS)
    return d * rstd, rstd


def padded(tile):
    tile = tile.astype(F32)
    parts = []
    for t in range(TROWS):
        rows = len(rows_of(t))
        parts += [tile[5 * t : 5 * t + rows].reshape(rows * TILE, C), jnp.zeros((128 - rows * TILE, C), F32)]
    return jnp.concatenate(parts, axis=0)


def compact(val):
    parts = [val[128 * t : 128 * t + TILE * len(rows_of(t))].reshape(-1, TILE, C) for t in range(TROWS)]
    return jnp.concatenate(parts, axis=0)


def first_kernel(pair_hbm, w_hbm, norm_hbm, send_ref, zn_ref, pair_ref, w_ref, norm_ref, sems):
    ends = ((pair_hbm, pair_ref), (norm_hbm, norm_ref), (w_hbm, w_ref))
    copies = [pltpu.make_async_copy(src, dst, sems.at[i]) for i, (src, dst) in enumerate(ends)]
    for copy in copies:
        copy.start()
    copies[0].wait()
    hat, _ = norm_lanes(pair_ref[...].astype(F32))
    copies[1].wait()
    zn = padded(hat * norm_ref[0:1, :][None] + norm_ref[1:2, :][None]).astype(BF16)
    zn_ref[...] = zn
    copies[2].wait()
    for m in range(2):
        p = dot(w_ref[:, 2 * m * C : (2 * m + 2) * C], zn, 0, 1)
        send_ref[:, m, :] = (jax.nn.sigmoid(p[C:]) * p[:C]).astype(BF16)


def block(src, q, row, t, first=0, rows=ROWS):
    return src[pl.ds(ROWS * q + first, rows), row, t * 128 : (t + 1) * 128].astype(F32)


def tile_of(row, per, t):
    return (row, t) if per == TROWS else (t // per, t % per)


def gather_rows(src, row, per, dst):
    wins = windows(ROWS)
    for g in range(2):
        for t in range(TROWS):
            parts = [block(src, 4 * g + u, *tile_of(row, per, t)) for u in range(4)]
            for i, o in zip(rows_of(t), spread_turn(parts, wins, t)):
                dst[pl.ds(16 * i, 16), g * 128 : (g + 1) * 128] = o.astype(BF16)


def scatter_rows(val, scr):
    wins = windows(ROWS)
    for g in range(2):
        for t in range(TROWS):
            parts = [val[16 * i : 16 * i + 16, g * 128 : (g + 1) * 128] for i in rows_of(t)]
            for u, o in enumerate(dense_turn(parts, wins)):
                scr[ROWS * (4 * g + u) : ROWS * (4 * g + u + 1), t * 128 : (t + 1) * 128] = o


def swap_blocks(val):
    pairs = val.reshape(-1, 2, WIDE, val.shape[1])
    return jnp.concatenate([pairs[:, 1:], pairs[:, :1]], axis=1).reshape(val.shape)


def gather_b(src, first, rows, bscr, b_dst):
    for n in range(2 * rows):
        bscr[pl.ds(n * WIDE + TILE, WIDE - TILE), :] = jnp.zeros((WIDE - TILE, 128), F32)
    wins = windows(rows)
    for g in range(2):
        for t in range(TROWS):
            parts = [block(src, 4 * g + u, 1, t, first, rows) for u in range(4)]
            for j, o in zip(rows_of(t), spread_turn(parts, wins, t)):
                bscr[pl.ds(rows * WIDE * g + j, rows, stride=WIDE), :] = o
        part = swap_blocks(bscr[rows * WIDE * g : rows * WIDE * (g + 1), :]).astype(BF16)
        b_dst[:, :, g * 128 : (g + 1) * 128] = part.reshape(rows // COLS, COLS * WIDE, 128)


def second_kernel(core_ref, src_ref, part_ref, a_ref, b_ref, bscr):
    gather_rows(src_ref, 0, TROWS, a_ref)
    gather_b(src_ref, 0, ROWS, bscr, b_ref)
    part_ref[...] = dot(a_ref[...], b_ref[core_ref[0]], 1, 1)


def second_kernel_sib(core_ref, src_ref, part_ref, send_ref, bscr, a_ref, b_ref, scr):
    gather_rows(src_ref, 0, TROWS, a_ref)
    gather_b(src_ref, COLS * core_ref[0], COLS, bscr, b_ref)
    scatter_rows(part_ref[...] + dot(a_ref[...], b_ref[0], 1, 1), scr)
    for t in range(TROWS):
        send_ref[:, t // 3, t % 3 * 128 : (t % 3 + 1) * 128] = scr[:, t * 128 : (t + 1) * 128].astype(BF16)
    send_ref[:, 1, 256:] = jnp.zeros((CHIPS, 128), BF16)


def column(row):
    return jnp.broadcast_to(row, (C, C)).T[:, :1]


def lane_sums(val):
    part = val[:, :128]
    for t in range(1, TROWS):
        part = part + val[:, t * 128 : (t + 1) * 128]
    return jnp.sum(part.T, axis=0, keepdims=True)


def third_kernel(recv_ref, zn_ref, cot_ref, w_ref, wo_ref, norm_ref, send_ref, upd_ref, dp4_ref, gwo_ref, mid_ref):
    x = jnp.concatenate([recv_ref[:, s, :].astype(F32) for s in range(2)], axis=1)[:, :POS]
    gain, bias = column(norm_ref[2:3, :]), column(norm_ref[3:4, :])
    mu = jnp.mean(x, axis=0, keepdims=True)
    d = x - mu
    rstd = 1.0 / jnp.sqrt(jnp.mean(d * d, axis=0, keepdims=True) + EPS)
    hat = d * rstd
    xn = (hat * gain + bias).astype(BF16)
    y = dot(wo_ref[...], xn, 0, 0)
    gate = jax.nn.sigmoid(dot(w_ref[:, 4 * C :], zn_ref[...], 0, 1))
    upd = compact((gate * y).T)
    upd_ref[...] = upd.astype(BF16)
    cot = padded(cot_ref[...]).T
    cg = cot * gate
    dy = cg.astype(BF16)
    dp4_ref[...] = (cg * y * (1.0 - gate)).astype(BF16)
    gwo_ref[...] = dot(xn, dy, 1, 1)
    dxn = dot(wo_ref[...], dy, 1, 0)
    mid_ref[0:1, :] = lane_sums(dxn * hat)
    mid_ref[1:2, :] = lane_sums(dxn)
    mid_ref[2:8, :] = jnp.zeros((6, 128), F32)
    e = dxn * gain
    dx = rstd * (e - jnp.mean(e, axis=0, keepdims=True) - hat * jnp.mean(e * hat, axis=0, keepdims=True))
    dx = jnp.concatenate([dx, jnp.zeros((C, 768 - POS), F32)], axis=1)
    for half in range(2):
        send_ref[:, half, :] = dx[:, half * 384 : (half + 1) * 384].astype(BF16)


def back_product(side, src, a_ref, b_ref, d_ref, dbscr, store):
    gather_rows(src, 0, 3, d_ref)
    dx = d_ref[...]
    db = dot(dx, a_ref[...], 0, 0)
    for g in range(2):
        dbscr[pl.ds(256 * g, 256), :] = swap_blocks(db[:, g * 128 : (g + 1) * 128])
    wins = windows(COLS)
    for g in range(2):
        for t in range(TROWS):
            parts = [dbscr[pl.ds(256 * g + j, COLS, stride=WIDE), :] for j in rows_of(t)]
            for u, o in enumerate(dense_turn(parts, wins)):
                store(4 * g + u, slice(t * 128, (t + 1) * 128), o)
    return dot(dx, b_ref[side], 1, 0)


def fourth_kernel(core_ref, src_ref, a_ref, b_ref, da_ref, db_ref, d_ref, dbscr):
    def store(q, lanes, val):
        db_ref[COLS * q : COLS * (q + 1), lanes] = val

    da_ref[...] = back_product(core_ref[0], src_ref, a_ref, b_ref, d_ref, dbscr, store)


def fourth_kernel_sib(core_ref, src_ref, a_ref, b_ref, da_ref, db_ref, send_ref, d_ref, dbscr, scr):
    core = core_ref[0]

    def store(q, lanes, val):
        scr[pl.ds(pl.multiple_of(ROWS * q + COLS * (1 - core), COLS), COLS), lanes] = val

    da = da_ref[...] + back_product(1 - core, src_ref, a_ref, b_ref, d_ref, dbscr, store)
    for q in range(COLS):
        scr[pl.ds(pl.multiple_of(ROWS * q + COLS * core, COLS), COLS), :] = db_ref[COLS * q : COLS * (q + 1), :]
    send_ref[:, 1, :] = scr[...].astype(BF16)
    scatter_rows(da, scr)
    send_ref[:, 0, :] = scr[...].astype(BF16)


def half_of(half, dp_ref, zn_ref, gwo_ref):
    grads = dot(dp_ref[pl.ds(pl.multiple_of(3 * C * half, 3 * C), 3 * C), :], zn_ref[...], 1, 0)
    last = grads[2 * C :] + jnp.where(half == 1, gwo_ref[...], 0.0)
    return jnp.concatenate([grads[: 2 * C], last], axis=0)


def fifth_kernel(core_ref, recv_ref, zn_ref, w_ref, dp4_ref, gwo_ref, give_ref, dp_ref):
    core = core_ref[0]
    zn = zn_ref[...]
    for m in range(2):
        grad = recv_ref[:, m, :].astype(F32)
        p = dot(w_ref[:, 2 * m * C : (2 * m + 2) * C], zn, 0, 1)
        s = jax.nn.sigmoid(p[C:])
        gs = grad * s
        dp_ref[2 * m * C : (2 * m + 1) * C, :] = gs.astype(BF16)
        dp_ref[(2 * m + 1) * C : (2 * m + 2) * C, :] = (gs * p[:C] * (1.0 - s)).astype(BF16)
    dp_ref[4 * C : 5 * C, :] = dp4_ref[...]
    dp_ref[5 * C :, :] = jnp.zeros((C, POS), BF16)
    give_ref[...] = half_of(1 - core, dp_ref, zn_ref, gwo_ref).astype(BF16)


def sixth_kernel(core_ref, dp_ref, zn_ref, gwo_ref, pair_ref, w_ref, mid_ref, norm_ref, gpair_ref, sums_ref, keep_ref):
    keep_ref[...] = half_of(core_ref[0], dp_ref, zn_ref, gwo_ref)
    dzn = dot(w_ref[...], dp_ref[: 5 * C, :], 1, 0).T
    hat, rstd = norm_lanes(padded(pair_ref[...]))
    e = dzn * norm_ref[0:1, :]
    back = rstd * (e - jnp.mean(e, axis=-1, keepdims=True) - hat * jnp.mean(e * hat, axis=-1, keepdims=True))
    gpair_ref[...] = compact(back).astype(BF16)
    first = jnp.sum(dzn * hat, axis=0, keepdims=True)
    second = jnp.sum(dzn, axis=0, keepdims=True)
    sums_ref[...] = jnp.concatenate([first, second, mid_ref[0:2, :], jnp.zeros((4, C), F32)], axis=0)


def join_kernel(keep_ref, sib_ref, sums_ref, send_ref):
    grads = (keep_ref[...] + sib_ref[...].astype(F32)).reshape(PLANE // 2, 24, C)
    sums = jnp.concatenate([sums_ref[...][None], jnp.zeros((PLANE // 2 - 1, 8, C), F32)], axis=0)
    send_ref[...] = jnp.concatenate([grads, sums], axis=1).astype(BF16)


def spread_kernel(recv_ref, send_ref, *, scale):
    total = jnp.sum(recv_ref[...].astype(F32), axis=0) * scale
    send_ref[...] = jnp.broadcast_to(total[None], send_ref.shape).astype(BF16)


def last_kernel(full_ref, upd_ref, gpair_ref, gwi_ref, gwo_ref, gn_ref, upd_out, gpair_out):
    upd_out[...] = upd_ref[...]
    gpair_out[...] = gpair_ref[...]
    full = full_ref[...].astype(F32).reshape(PLANE // 2, 2, 32, C)
    halves = [full[:, h, :24, :].reshape(3 * C, C) for h in range(2)]
    for m in range(5):
        gwi_ref[:, m * C : (m + 1) * C] = halves[m // 3][m % 3 * C : (m % 3 + 1) * C, :].T
    gwo_ref[...] = halves[1][2 * C :, :]
    gn_ref[...] = full[0, 0, 24:28, :] + full[0, 1, 24:28, :]


def call(kernel, outs, scratch, *args, scalars=0, far=False):
    vmem = pl.BlockSpec(memory_space=pltpu.VMEM)
    smem = pl.BlockSpec(memory_space=pltpu.SMEM)
    rest = pl.BlockSpec(memory_space=pltpu.HBM) if far else vmem
    return pl.pallas_call(
        kernel,
        out_shape=[jax.ShapeDtypeStruct(s, t) for s, t in outs],
        in_specs=[smem] * scalars + [rest] * (len(args) - scalars),
        out_specs=[vmem] * len(outs),
        scratch_shapes=scratch,
        compiler_params=pltpu.CompilerParams(vmem_limit_bytes=40 * 1024 * 1024),
    )(*args)


def shards(pair, cotangent, w_in, w_out, norm_params):
    swap = [(0, 1), (1, 0)]
    f32, bf16 = (lambda *s: pltpu.VMEM(s, F32)), (lambda *s: pltpu.VMEM(s, BF16))
    wide, thin = ((CHIPS, 2, POS), BF16), ((CHIPS, 2, 384), BF16)

    chunks = ((PLANE, 32, C), BF16)

    def turn(x, axes=CHIP_AXES):
        flip = 0
        for axis in axes:
            flip = flip * lax.axis_size(axis) + FLIPS.get(axis, 0)
        groups = [[n ^ flip for n in range(x.shape[0])]]
        return lax.all_to_all(x, axes, split_axis=0, concat_axis=0, axis_index_groups=groups, tiled=True)

    core = lax.axis_index("core").astype(jnp.int32).reshape(1)
    send, zn = call(
        first_kernel,
        [wide, ((POS, C), BF16)],
        [bf16(TILE, TILE, C), bf16(C, 5 * C), f32(4, C), pltpu.SemaphoreType.DMA((3,))],
        *[pltpu.with_memory_space_constraint(v, pltpu.HBM) for v in (pair, w_in, norm_params)],
        far=True,
    )
    own = turn(send)
    sib = lax.ppermute(own, "core", swap)
    part, a_own, b_own = call(
        second_kernel,
        [((384, 256), F32), ((384, 256), BF16), ((2, COLS * WIDE, 256), BF16)],
        [f32(1024 + WIDE, 128)],
        core,
        own,
        scalars=1,
    )
    (send,) = call(
        second_kernel_sib,
        [thin],
        [f32(512 + WIDE, 128), bf16(384, 256), bf16(1, COLS * WIDE, 256), f32(CHIPS, POS)],
        core,
        sib,
        part,
        scalars=1,
    )
    send, update, dp4, gwo, mid = call(
        third_kernel,
        [thin, ((TILE, TILE, C), BF16), ((C, POS), BF16), ((C, C), F32), ((8, 128), F32)],
        [],
        turn(send),
        zn,
        cotangent,
        w_in,
        w_out,
        norm_params,
    )
    own = turn(send)
    sib = lax.ppermute(own, "core", swap)
    scratch = [bf16(384, 256), f32(512 + WIDE, 128)]
    da, db = call(
        fourth_kernel,
        [((384, 256), F32), ((CHIPS // 2, POS), F32)],
        scratch,
        core,
        own,
        a_own,
        b_own,
        scalars=1,
    )
    (send,) = call(
        fourth_kernel_sib, [wide], scratch + [f32(CHIPS, POS)], core, sib, a_own, b_own, da, db, scalars=1
    )
    give, dp = call(
        fifth_kernel,
        [((3 * C, C), BF16), ((6 * C, POS), BF16)],
        [],
        core,
        turn(send),
        zn,
        w_in,
        dp4,
        gwo,
        scalars=1,
    )
    sib = lax.ppermute(give, "core", swap)
    grad_pair, sums, keep = call(
        sixth_kernel,
        [((TILE, TILE, C), BF16), ((8, C), F32), ((3 * C, C), F32)],
        [],
        core,
        dp,
        zn,
        gwo,
        pair,
        w_in,
        mid,
        norm_params,
        scalars=1,
    )
    (send,) = call(join_kernel, [((PLANE // 2, 32, C), BF16)], [], keep, sib, sums)
    send = turn(send, PLANE_AXES[:3])
    (send,) = call(functools.partial(spread_kernel, scale=1.0), [((8, 32, C), BF16)], [], send)
    (send,) = call(functools.partial(spread_kernel, scale=1.0 / 384.0), [chunks], [], turn(send, ("z",)))
    tile = ((TILE, TILE, C), BF16)
    grad_w_in, grad_w_out, grad_norm, update, grad_pair = call(
        last_kernel,
        [((C, 5 * C), F32), ((C, C), F32), ((4, C), F32), tile, tile],
        [],
        turn(send, PLANE_AXES),
        update,
        grad_pair,
    )
    return (update, grad_pair, grad_w_in, grad_w_out, grad_norm)


def solution(mesh):
    fine = Mesh(mesh.devices.reshape(8, 2, 4, 2, 2), ("z", "yl", "x", "yh", "core"))
    tile = P(("z", "yl"), ("x", "yh", "core"), None)
    placed = (tile, tile, P(), P(), P())
    return jax.shard_map(shards, mesh=fine, in_specs=placed, out_specs=placed, check_vma=False)
```

```python
import functools

import jax
import jax.numpy as jnp
from jax import lax
from jax.experimental import pallas as pl
from jax.experimental.pallas import tpu as pltpu
from jax.sharding import Mesh
from jax.sharding import PartitionSpec as P

F32 = jnp.float32
BF16 = jnp.bfloat16
EPS = 1e-05
ROWS = 16
COLS = 8
CHIPS = 128
TILE = 24
WIDE = 32
TROWS = 5
POS = 128 * TROWS
C = 128
PLANE = 32
CHIP_AXES = ("x", "yh", "yl", "z")
PLANE_AXES = ("yl", "x", "yh", "core")
FLIPS = {"x": 2, "yh": 1, "z": 5}


def dot(x, y, cx, cy):
    return lax.dot_general(x, y, (((cx,), (cy,)), ((), ())), preferred_element_type=F32)


def windows(rows):
    lane = lax.broadcasted_iota(jnp.int32, (rows, 128), 1)
    return lane, [((lane - 8 * n) & 127) < TILE for n in range(16)]


def block_turn(parts, wins, step, count, out_step, used):
    lane, masks = wins
    rolled = [p if a == 0 else pltpu.roll(p, step * a % 128, 1) for a, p in enumerate(parts)]
    outs = []
    for b in range(count):
        mixed = rolled[0]
        for a in range(1, len(parts)):
            mixed = jnp.where(masks[(step * a + out_step * b) % 128 // 8], rolled[a], mixed)
        if b:
            mixed = pltpu.roll(mixed, (128 - out_step * b) % 128, 1)
        outs.append(jnp.where(used, mixed, 0.0))
    return outs


def spread_turn(parts, wins, t):
    return block_turn(parts, wins, WIDE, min(5, TILE - 5 * t), TILE, (wins[0] & 31) < TILE)


def dense_turn(parts, wins):
    return block_turn(parts, wins, TILE, 4, WIDE, wins[0] < TILE * len(parts))


def rows_of(t):
    return range(5 * t, min(5 * t + 5, TILE))


def norm_lanes(v):
    mu = jnp.mean(v, axis=-1, keepdims=True)
    d = v - mu
    rstd = 1.0 / jnp.sqrt(jnp.mean(d * d, axis=-1, keepdims=True) + EPS)
    return d * rstd, rstd


def padded(tile):
    tile = tile.astype(F32)
    parts = []
    for t in range(TROWS):
        rows = len(rows_of(t))
        parts += [tile[5 * t : 5 * t + rows].reshape(rows * TILE, C), jnp.zeros((128 - rows * TILE, C), F32)]
    return jnp.concatenate(parts, axis=0)


def compact(val):
    parts = [val[128 * t : 128 * t + TILE * len(rows_of(t))].reshape(-1, TILE, C) for t in range(TROWS)]
    return jnp.concatenate(parts, axis=0)


def first_kernel(pair_hbm, w_hbm, norm_hbm, send_ref, zn_ref, pair_ref, w_ref, norm_ref, sems):
    ends = ((pair_hbm, pair_ref), (norm_hbm, norm_ref), (w_hbm, w_ref))
    copies = [pltpu.make_async_copy(src, dst, sems.at[i]) for i, (src, dst) in enumerate(ends)]
    for copy in copies:
        copy.start()
    copies[0].wait()
    hat, _ = norm_lanes(pair_ref[...].astype(F32))
    copies[1].wait()
    zn = padded(hat * norm_ref[0:1, :][None] + norm_ref[1:2, :][None]).astype(BF16)
    zn_ref[...] = zn
    copies[2].wait()
    for m in range(2):
        p = dot(w_ref[:, 2 * m * C : (2 * m + 2) * C], zn, 0, 1)
        send_ref[:, m, :] = (jax.nn.sigmoid(p[C:]) * p[:C]).astype(BF16)


def block(src, q, row, t, first=0, rows=ROWS):
    return src[pl.ds(ROWS * q + first, rows), row, t * 128 : (t + 1) * 128].astype(F32)


def tile_of(row, per, t):
    return (row, t) if per == TROWS else (t // per, t % per)


def gather_rows(src, row, per, dst):
    wins = windows(ROWS)
    for g in range(2):
        for t in range(TROWS):
            parts = [block(src, 4 * g + u, *tile_of(row, per, t)) for u in range(4)]
            for i, o in zip(rows_of(t), spread_turn(parts, wins, t)):
                dst[pl.ds(16 * i, 16), g * 128 : (g + 1) * 128] = o.astype(BF16)


def scatter_rows(val, scr):
    wins = windows(ROWS)
    for g in range(2):
        for t in range(TROWS):
            parts = [val[16 * i : 16 * i + 16, g * 128 : (g + 1) * 128] for i in rows_of(t)]
            for u, o in enumerate(dense_turn(parts, wins)):
                scr[ROWS * (4 * g + u) : ROWS * (4 * g + u + 1), t * 128 : (t + 1) * 128] = o


def gather_b(src, first, rows, bscr, b_dst):
    for n in range(2 * rows):
        bscr[pl.ds(n * WIDE + TILE, WIDE - TILE), :] = jnp.zeros((WIDE - TILE, 128), F32)
    wins = windows(rows)
    for g in range(2):
        for t in range(TROWS):
            parts = [block(src, 4 * g + u, 1, t, first, rows) for u in range(4)]
            for j, o in zip(rows_of(t), spread_turn(parts, wins, t)):
                bscr[pl.ds(rows * WIDE * g + j, rows, stride=WIDE), :] = o
        part = bscr[rows * WIDE * g : rows * WIDE * (g + 1), :].astype(BF16)
        b_dst[:, :, g * 128 : (g + 1) * 128] = part.reshape(rows // COLS, COLS * WIDE, 128)


def second_kernel(core_ref, src_ref, part_ref, a_ref, b_ref, bscr):
    gather_rows(src_ref, 0, TROWS, a_ref)
    gather_b(src_ref, 0, ROWS, bscr, b_ref)
    part_ref[...] = dot(a_ref[...], b_ref[core_ref[0]], 1, 1)


def second_kernel_sib(core_ref, src_ref, part_ref, send_ref, bscr, a_ref, b_ref, scr):
    gather_rows(src_ref, 0, TROWS, a_ref)
    gather_b(src_ref, COLS * core_ref[0], COLS, bscr, b_ref)
    scatter_rows(part_ref[...] + dot(a_ref[...], b_ref[0], 1, 1), scr)
    for t in range(TROWS):
        send_ref[:, t // 3, t % 3 * 128 : (t % 3 + 1) * 128] = scr[:, t * 128 : (t + 1) * 128].astype(BF16)
    send_ref[:, 1, 256:] = jnp.zeros((CHIPS, 128), BF16)


def column(row):
    return jnp.broadcast_to(row, (C, C)).T[:, :1]


def lane_sums(val):
    part = val[:, :128]
    for t in range(1, TROWS):
        part = part + val[:, t * 128 : (t + 1) * 128]
    return jnp.sum(part.T, axis=0, keepdims=True)


def third_kernel(recv_ref, zn_ref, cot_ref, w_ref, wo_ref, norm_ref, send_ref, upd_ref, dp4_ref, gwo_ref, mid_ref):
    x = jnp.concatenate([recv_ref[:, s, :].astype(F32) for s in range(2)], axis=1)[:, :POS]
    gain, bias = column(norm_ref[2:3, :]), column(norm_ref[3:4, :])
    mu = jnp.mean(x, axis=0, keepdims=True)
    d = x - mu
    rstd = 1.0 / jnp.sqrt(jnp.mean(d * d, axis=0, keepdims=True) + EPS)
    hat = d * rstd
    xn = (hat * gain + bias).astype(BF16)
    y = dot(wo_ref[...], xn, 0, 0)
    gate = jax.nn.sigmoid(dot(w_ref[:, 4 * C :], zn_ref[...], 0, 1))
    upd = compact((gate * y).T)
    upd_ref[...] = upd.astype(BF16)
    cot = padded(cot_ref[...]).T
    cg = cot * gate
    dy = cg.astype(BF16)
    dp4_ref[...] = (cg * y * (1.0 - gate)).astype(BF16)
    gwo_ref[...] = dot(xn, dy, 1, 1)
    dxn = dot(wo_ref[...], dy, 1, 0)
    mid_ref[0:1, :] = lane_sums(dxn * hat)
    mid_ref[1:2, :] = lane_sums(dxn)
    mid_ref[2:8, :] = jnp.zeros((6, 128), F32)
    e = dxn * gain
    dx = rstd * (e - jnp.mean(e, axis=0, keepdims=True) - hat * jnp.mean(e * hat, axis=0, keepdims=True))
    dx = jnp.concatenate([dx, jnp.zeros((C, 768 - POS), F32)], axis=1)
    for half in range(2):
        send_ref[:, half, :] = dx[:, half * 384 : (half + 1) * 384].astype(BF16)


def back_product(side, src, a_ref, b_ref, d_ref, dbscr, store):
    gather_rows(src, 0, 3, d_ref)
    dx = d_ref[...]
    db = dot(dx, a_ref[...], 0, 0)
    for g in range(2):
        dbscr[pl.ds(256 * g, 256), :] = db[:, g * 128 : (g + 1) * 128]
    wins = windows(COLS)
    for g in range(2):
        for t in range(TROWS):
            parts = [dbscr[pl.ds(256 * g + j, COLS, stride=WIDE), :] for j in rows_of(t)]
            for u, o in enumerate(dense_turn(parts, wins)):
                store(4 * g + u, slice(t * 128, (t + 1) * 128), o)
    return dot(dx, b_ref[side], 1, 0)


def fourth_kernel(core_ref, src_ref, a_ref, b_ref, da_ref, db_ref, d_ref, dbscr):
    def store(q, lanes, val):
        db_ref[COLS * q : COLS * (q + 1), lanes] = val

    da_ref[...] = back_product(core_ref[0], src_ref, a_ref, b_ref, d_ref, dbscr, store)


def fourth_kernel_sib(core_ref, src_ref, a_ref, b_ref, da_ref, db_ref, send_ref, d_ref, dbscr, scr):
    core = core_ref[0]

    def store(q, lanes, val):
        scr[pl.ds(pl.multiple_of(ROWS * q + COLS * (1 - core), COLS), COLS), lanes] = val

    da = da_ref[...] + back_product(1 - core, src_ref, a_ref, b_ref, d_ref, dbscr, store)
    for q in range(COLS):
        scr[pl.ds(pl.multiple_of(ROWS * q + COLS * core, COLS), COLS), :] = db_ref[COLS * q : COLS * (q + 1), :]
    send_ref[:, 1, :] = scr[...].astype(BF16)
    scatter_rows(da, scr)
    send_ref[:, 0, :] = scr[...].astype(BF16)


def fifth_kernel(core_ref, recv_ref, zn_ref, w_ref, dp4_ref, gwo_ref, keep_ref, give_ref, dp_ref, scr):
    core = core_ref[0]
    zn = zn_ref[...]
    for m in range(2):
        grad = recv_ref[:, m, :].astype(F32)
        p = dot(w_ref[:, 2 * m * C : (2 * m + 2) * C], zn, 0, 1)
        s = jax.nn.sigmoid(p[C:])
        gs = grad * s
        dp_ref[2 * m * C : (2 * m + 1) * C, :] = gs.astype(BF16)
        dp_ref[(2 * m + 1) * C : (2 * m + 2) * C, :] = (gs * p[:C] * (1.0 - s)).astype(BF16)
    dp_ref[4 * C :, :] = dp4_ref[...]
    grads = dot(dp_ref[...], zn, 1, 0)
    scr[0] = grads[: 3 * C]
    scr[1, : 2 * C, :] = grads[3 * C :]
    scr[1, 2 * C :, :] = gwo_ref[...]
    keep_ref[...] = scr[core]
    give_ref[...] = scr[1 - core]


def sixth_kernel(dp_ref, pair_ref, w_ref, mid_ref, norm_ref, gpair_ref, sums_ref):
    dzn = dot(w_ref[...], dp_ref[...], 1, 0).T
    hat, rstd = norm_lanes(padded(pair_ref[...]))
    e = dzn * norm_ref[0:1, :]
    back = rstd * (e - jnp.mean(e, axis=-1, keepdims=True) - hat * jnp.mean(e * hat, axis=-1, keepdims=True))
    gpair_ref[...] = compact(back).astype(BF16)
    first = jnp.sum(dzn * hat, axis=0, keepdims=True)
    second = jnp.sum(dzn, axis=0, keepdims=True)
    sums_ref[...] = jnp.concatenate([first, second, mid_ref[0:2, :], jnp.zeros((4, C), F32)], axis=0)


def join_kernel(keep_ref, sib_ref, sums_ref, send_ref):
    grads = (keep_ref[...] + sib_ref[...]).reshape(PLANE // 2, 24, C)
    sums = jnp.concatenate([sums_ref[...][None], jnp.zeros((PLANE // 2 - 1, 8, C), F32)], axis=0)
    send_ref[...] = jnp.concatenate([grads, sums], axis=1).astype(BF16)


def spread_kernel(recv_ref, send_ref, *, scale):
    total = jnp.sum(recv_ref[...].astype(F32), axis=0) * scale
    send_ref[...] = jnp.broadcast_to(total[None], send_ref.shape).astype(BF16)


def last_kernel(full_ref, upd_ref, gpair_ref, gwi_ref, gwo_ref, gn_ref, upd_out, gpair_out):
    upd_out[...] = upd_ref[...]
    gpair_out[...] = gpair_ref[...]
    full = full_ref[...].astype(F32).reshape(PLANE // 2, 2, 32, C)
    halves = [full[:, h, :24, :].reshape(3 * C, C) for h in range(2)]
    for m in range(5):
        gwi_ref[:, m * C : (m + 1) * C] = halves[m // 3][m % 3 * C : (m % 3 + 1) * C, :].T
    gwo_ref[...] = halves[1][2 * C :, :]
    gn_ref[...] = full[0, 0, 24:28, :] + full[0, 1, 24:28, :]


def call(kernel, outs, scratch, *args, scalars=0, far=False):
    vmem = pl.BlockSpec(memory_space=pltpu.VMEM)
    smem = pl.BlockSpec(memory_space=pltpu.SMEM)
    rest = pl.BlockSpec(memory_space=pltpu.HBM) if far else vmem
    return pl.pallas_call(
        kernel,
        out_shape=[jax.ShapeDtypeStruct(s, t) for s, t in outs],
        in_specs=[smem] * scalars + [rest] * (len(args) - scalars),
        out_specs=[vmem] * len(outs),
        scratch_shapes=scratch,
        compiler_params=pltpu.CompilerParams(vmem_limit_bytes=40 * 1024 * 1024),
    )(*args)


def shards(pair, cotangent, w_in, w_out, norm_params):
    swap = [(0, 1), (1, 0)]
    f32, bf16 = (lambda *s: pltpu.VMEM(s, F32)), (lambda *s: pltpu.VMEM(s, BF16))
    wide, thin = ((CHIPS, 2, POS), BF16), ((CHIPS, 2, 384), BF16)

    chunks = ((PLANE, 32, C), BF16)

    def turn(x, axes=CHIP_AXES):
        flip = 0
        for axis in axes:
            flip = flip * lax.axis_size(axis) + FLIPS.get(axis, 0)
        groups = [[n ^ flip for n in range(x.shape[0])]]
        return lax.all_to_all(x, axes, split_axis=0, concat_axis=0, axis_index_groups=groups, tiled=True)

    core = lax.axis_index("core").astype(jnp.int32).reshape(1)
    send, zn = call(
        first_kernel,
        [wide, ((POS, C), BF16)],
        [bf16(TILE, TILE, C), bf16(C, 5 * C), f32(4, C), pltpu.SemaphoreType.DMA((3,))],
        *[pltpu.with_memory_space_constraint(v, pltpu.HBM) for v in (pair, w_in, norm_params)],
        far=True,
    )
    own = turn(send)
    sib = lax.ppermute(own, "core", swap)
    part, a_own, b_own = call(
        second_kernel,
        [((384, 256), F32), ((384, 256), BF16), ((2, COLS * WIDE, 256), BF16)],
        [f32(1024 + WIDE, 128)],
        core,
        own,
        scalars=1,
    )
    (send,) = call(
        second_kernel_sib,
        [thin],
        [f32(512 + WIDE, 128), bf16(384, 256), bf16(1, COLS * WIDE, 256), f32(CHIPS, POS)],
        core,
        sib,
        part,
        scalars=1,
    )
    send, update, dp4, gwo, mid = call(
        third_kernel,
        [thin, ((TILE, TILE, C), BF16), ((C, POS), BF16), ((C, C), F32), ((8, 128), F32)],
        [],
        turn(send),
        zn,
        cotangent,
        w_in,
        w_out,
        norm_params,
    )
    own = turn(send)
    sib = lax.ppermute(own, "core", swap)
    scratch = [bf16(384, 256), f32(512 + WIDE, 128)]
    da, db = call(
        fourth_kernel,
        [((384, 256), F32), ((CHIPS // 2, POS), F32)],
        scratch,
        core,
        own,
        a_own,
        b_own,
        scalars=1,
    )
    (send,) = call(
        fourth_kernel_sib, [wide], scratch + [f32(CHIPS, POS)], core, sib, a_own, b_own, da, db, scalars=1
    )
    half = ((3 * C, C), F32)
    keep, give, dp = call(
        fifth_kernel,
        [half, half, ((5 * C, POS), BF16)],
        [f32(2, 3 * C, C)],
        core,
        turn(send),
        zn,
        w_in,
        dp4,
        gwo,
        scalars=1,
    )
    sib = lax.ppermute(give, "core", swap)
    grad_pair, sums = call(
        sixth_kernel, [((TILE, TILE, C), BF16), ((8, C), F32)], [], dp, pair, w_in, mid, norm_params
    )
    (send,) = call(join_kernel, [((PLANE // 2, 32, C), BF16)], [], keep, sib, sums)
    send = turn(send, PLANE_AXES[:3])
    (send,) = call(functools.partial(spread_kernel, scale=1.0), [((8, 32, C), BF16)], [], send)
    (send,) = call(functools.partial(spread_kernel, scale=1.0 / 384.0), [chunks], [], turn(send, ("z",)))
    tile = ((TILE, TILE, C), BF16)
    grad_w_in, grad_w_out, grad_norm, update, grad_pair = call(
        last_kernel,
        [((C, 5 * C), F32), ((C, C), F32), ((4, C), F32), tile, tile],
        [],
        turn(send, PLANE_AXES),
        update,
        grad_pair,
    )
    return (update, grad_pair, grad_w_in, grad_w_out, grad_norm)


def solution(mesh):
    fine = Mesh(mesh.devices.reshape(8, 2, 4, 2, 2), ("z", "yl", "x", "yh", "core"))
    tile = P(("z", "yl"), ("x", "yh", "core"), None)
    placed = (tile, tile, P(), P(), P())
    return jax.shard_map(shards, mesh=fine, in_specs=placed, out_specs=placed, check_vma=False)
```
